32 devices in a mesh: parts: 2 (over x), seg: 2 (over core), tile: 8 (over z, y).
Axes of the slice: x: 2, y: 2, z: 4, core: 2. Of those that a mesh axis runs over, the one named last changes fastest.
Arguments:
- psi: float32 [4, 8, 128, 128], P(('parts', 'seg'), 'tile'), parts along dimension 0, may hold values from -162 to 162
- left_env: float32 [4, 128, 128, 128], P(('parts', 'seg'), 'tile'), parts along dimension 0, may hold values from -6 to 6
- right_env: float32 [4, 128, 128, 128], P(('parts', 'seg'), 'tile'), parts along dimension 0, may hold values from -6 to 6
- site_energy: float32 [4, 8], P(('parts', 'seg')), parts along dimension 0, may hold values from 1 to 4
- mv_counts: int32 [4, 8, 16], P(('parts', 'seg'), 'tile'), parts along dimension 0, may hold values from 1 to 24, 192 in all within a row
- mv_src: int32 [4, 8, 192], P(('parts', 'seg'), 'tile'), parts along dimension 0, may hold values from 0 to 7
- mv_dst: int32 [4, 8, 192], P(('parts', 'seg'), 'tile'), parts along dimension 0, may hold values from 0 to 7
- mv_coef: float32 [4, 8, 192], P(('parts', 'seg'), 'tile'), parts along dimension 0, may hold values from -0.01171875 to 0.01171875
- up_counts: int32 [4, 8, 16], P(('parts', 'seg'), 'tile'), parts along dimension 0, may hold values from 1 to 24, 192 in all within a row
- up_block: int32 [4, 8, 192], P(('parts', 'seg'), 'tile'), parts along dimension 0, may hold values from 0 to 15
- up_top: int32 [4, 8, 192], P(('parts', 'seg'), 'tile'), parts along dimension 0, may hold values from 0 to 7
- up_bot: int32 [4, 8, 192], P(('parts', 'seg'), 'tile'), parts along dimension 0, may hold values from 0 to 7
- up_coef: float32 [4, 8, 192], P(('parts', 'seg'), 'tile'), parts along dimension 0, may hold values from -0.005859375 to 0.005859375
Outputs:
- residual: float32 [4, 8, 128, 128], P(('parts', 'seg'), 'tile'), parts along dimension 0
- renewed: float32 [4, 128, 128, 128], P(('parts', 'seg'), 'tile'), parts along dimension 0
- rayleigh: float32 [4], P(('parts', 'seg')), parts along dimension 0
The draws below stay inside these ranges and needn't reach their ends.
There are 2 independent parts, one for each index of `parts`. The reference program is written for one: setup_inputs(seed, part) draws one part's arguments, and reference() takes and returns one part's arrays. A program takes and returns all parts, laid end to end along the dimension named above; each array names one. Nothing has to cross between parts.
Inputs may be any that keep to these rules, and one draw needn't show every extreme that they name: `mv_counts`: on every tile index the counts of its 16 channels add up to 192, and one channel of each tile index has exactly 24. `up_counts`: on every tile index the counts of its 16 channels add up to 192, and one channel of each tile index has exactly 24.
All inputs are finite; a program needn't handle non-finite values.
Results may differ from the reference program's by a relative error of at most 0.0003.
Values sent between devices are 32-bit elements; how exact they have to be, the bound alone decides.
No kernel may reach another device: no remote copies, remote signals or barrier semaphores. Data moves between devices by JAX's collectives and lax.ppermute only.
A program may use at most 64 MiB of HBM per device.

```python
import math
import jax
import jax.numpy as jnp
import numpy as np
from jax import lax

BW = 128
ENV_DEV = 16
MAXT = 24
SEGS = 2
GROUP = 8
NPSI = 8
NENV = 128
LIVE = 192


def draw_psi(key, part):
    key = jax.random.fold_in(key, 17)
    base_key, row_key, col_key = jax.random.split(key, 3)
    array_shape = (SEGS, NPSI, BW, BW)
    values = jnp.clip(jax.random.normal(base_key, array_shape, jnp.float32), -6.0, 6.0)
    row_scale = jnp.exp(jax.random.uniform(row_key, (SEGS, NPSI, BW, 1), jnp.float32, math.log(0.3), math.log(3.0)))
    col_scale = jnp.exp(jax.random.uniform(col_key, (SEGS, NPSI, 1, BW), jnp.float32, math.log(0.3), math.log(3.0)))
    tile_ramp = 1.0 + 2.0 * jnp.arange(NPSI, dtype=jnp.float32) / max(NPSI - 1, 1)
    return values * row_scale * col_scale * tile_ramp[None, :, None, None]


def with_ends(values, stream_key, low, largest):
    spot = [jax.random.randint(jax.random.fold_in(stream_key, axis), (), 0, length) for axis, length in enumerate(values.shape)]
    longest = values.shape.index(max(values.shape))
    next_to = spot[:longest] + [(spot[longest] + 1) % values.shape[longest]] + spot[longest + 1:]
    return values.at[tuple(spot)].set(low).at[tuple(next_to)].set(largest)


def levels(key, dims, cuts, smallest, top_value):
    loudness, own = 1.0, jax.random.fold_in(key, 6)
    for position, shards_of in cuts:
        steps = jnp.exp(jax.random.uniform(jax.random.fold_in(own, position), (shards_of,), jnp.float32, smallest / len(cuts), top_value / len(cuts)))
        loudness = loudness * jnp.repeat(steps, dims[position] // shards_of).reshape([-1 if axis == position else 1 for axis in range(len(dims))])
    return loudness


def profile(number_of, total, most, skew):
    loads = [(1 << 20) // math.isqrt(standing ** skew) + 1 for standing in range(2, number_of + 1)]
    rest, holding = total - most - (number_of - 1), [1] * (number_of - 1)
    while rest > 0:
        candidates = [i for i in range(number_of - 1) if holding[i] < most]
        pool, remaining = sum([loads[i] for i in candidates]), rest
        for i in candidates:
            addition = min(most - holding[i], max(1, remaining * loads[i] // pool), rest)
            holding[i] = holding[i] + addition
            rest = rest - addition
    return np.array([most] + holding)


def ragged(rng, number_of, total, limit, skew):
    if number_of == 2:
        one = jax.random.randint(rng, (), max(1, total - limit), min(limit, total - 1) + 1)
        return jnp.stack([one, total - one])
    lengths = jnp.asarray(profile(number_of, total, limit, skew), jnp.int32)
    couples = (number_of - 1) // 2
    source_of, receiver = lengths[1:1 + 2 * couples:2], lengths[2:2 + 2 * couples:2]
    slack = jnp.minimum(source_of - 1, limit - receiver)
    shifted = jax.random.randint(jax.random.fold_in(rng, 1), (couples,), 0, 1 << 20) % (slack + 1)
    lengths = lengths.at[1:1 + 2 * couples:2].set(source_of - shifted).at[2:2 + 2 * couples:2].set(receiver + shifted)
    return lengths[jax.random.permutation(jax.random.fold_in(rng, 2), number_of)]


def normal_values(own_key, extent, deviation, bound, cuts=(), kind=jnp.bfloat16):
    values = deviation * jax.random.normal(own_key, extent, jnp.float32)
    if cuts:
        values = values * levels(own_key, extent, cuts, -0.22, 0.18)
    return jnp.clip(values, -bound, bound).astype(kind)


def setup_inputs(seed: int = 0, part: int = 0) -> dict:
    key_of = jax.random.split(jax.random.key(seed), 14)
    own_keys = jax.random.split(jax.random.fold_in(key_of[13], part), 14)
    psi = draw_psi(jax.random.fold_in(jax.random.fold_in(key_of[13], part), 71), part)
    left_env = normal_values(own_keys[1], (SEGS, NENV, BW, BW), 1.0, 6.0, ((0, 2), (1, 8)), jnp.float32)
    right_env = normal_values(own_keys[2], (SEGS, NENV, BW, BW), 1.0, 6.0, ((0, 2), (1, 8)), jnp.float32)
    site_energy = jnp.clip(1.0 + 3.0 * jax.random.uniform(own_keys[3], (SEGS, NPSI), jnp.float32) ** levels(own_keys[3], (SEGS, NPSI), ((0, 2),), -0.2, 0.2), 1.0, 4.0)
    mv_counts = jax.vmap(lambda own: ragged(own, ENV_DEV, LIVE, MAXT, 2))(jax.random.split(own_keys[4], SEGS * GROUP)).reshape((SEGS, GROUP, ENV_DEV)).astype(jnp.int32)
    mv_src = with_ends(jax.random.randint(own_keys[5], (SEGS, GROUP, LIVE), 0, NPSI), jax.random.fold_in(own_keys[5], 1), 0, NPSI - 1).astype(jnp.int32)
    mv_dst = with_ends(jax.random.randint(own_keys[6], (SEGS, GROUP, LIVE), 0, NPSI), jax.random.fold_in(own_keys[6], 1), 0, NPSI - 1).astype(jnp.int32)
    mv_coef = normal_values(own_keys[7], (SEGS, GROUP, LIVE), (0.1 / BW), 0.01171875, ((0, 2), (1, 8)), jnp.float32)
    up_counts = jax.vmap(lambda own: ragged(own, ENV_DEV, LIVE, MAXT, 2))(jax.random.split(own_keys[8], SEGS * GROUP)).reshape((SEGS, GROUP, ENV_DEV)).astype(jnp.int32)
    up_block = with_ends(jax.random.randint(own_keys[9], (SEGS, GROUP, LIVE), 0, ENV_DEV), jax.random.fold_in(own_keys[9], 1), 0, ENV_DEV - 1).astype(jnp.int32)
    up_top = with_ends(jax.random.randint(own_keys[10], (SEGS, GROUP, LIVE), 0, NPSI), jax.random.fold_in(own_keys[10], 1), 0, NPSI - 1).astype(jnp.int32)
    up_bot = with_ends(jax.random.randint(own_keys[11], (SEGS, GROUP, LIVE), 0, NPSI), jax.random.fold_in(own_keys[11], 1), 0, NPSI - 1).astype(jnp.int32)
    up_coef = normal_values(own_keys[12], (SEGS, GROUP, LIVE), (0.05 / BW), 0.005859375, ((0, 2), (1, 8)), jnp.float32)
    return dict(psi=psi, left_env=left_env, right_env=right_env, site_energy=site_energy, mv_counts=mv_counts, mv_src=mv_src, mv_dst=mv_dst, mv_coef=mv_coef, up_counts=up_counts, up_block=up_block, up_top=up_top, up_bot=up_bot, up_coef=up_coef)


def channel_index(counts, live_count):
    block_ends = jnp.cumsum(counts).astype(jnp.int32)
    positions = jnp.arange(live_count, dtype=jnp.int32)
    return jnp.sum((positions[:, None] >= block_ends[None, :]).astype(jnp.int32), axis=1).astype(jnp.int32)


def tile_product(left, right):
    return jnp.einsum("eij,ejk->eik", left, right, precision=lax.Precision.HIGHEST)


def renew_segment(psi_seg, env_seg, counts, blocks, tops, bottoms, coefs):
    def one_group(inputs):
        env_group, count_row, block_row, top_row, bottom_row, coef_row = inputs
        targets = channel_index(count_row, LIVE)
        inner = tile_product(env_group[block_row], psi_seg[bottom_row])
        contrib = jnp.einsum("eji,ejk->eik", psi_seg[top_row], inner, precision=lax.Precision.HIGHEST)
        contrib = contrib * coef_row[:, None, None]
        return jax.ops.segment_sum(contrib, targets, num_segments=ENV_DEV)

    grouped = env_seg.reshape(GROUP, ENV_DEV, BW, BW)
    result = lax.map(one_group, (grouped, counts, blocks, tops, bottoms, coefs))
    return result.reshape(NENV, BW, BW)


def apply_segment(psi_seg, env_seg, right_seg, counts, sources, targets, coefs):
    def one_group(running, inputs):
        env_group, right_group, count_row, source_row, target_row, coef_row = inputs
        channels = channel_index(count_row, LIVE)
        inner = tile_product(psi_seg[source_row], right_group[channels])
        contrib = tile_product(env_group[channels], inner) * coef_row[:, None, None]
        return running + jax.ops.segment_sum(contrib, target_row, num_segments=NPSI), None

    inputs = (env_seg.reshape(GROUP, ENV_DEV, BW, BW), right_seg.reshape(GROUP, ENV_DEV, BW, BW),
              counts, sources, targets, coefs)
    summed, unused = lax.scan(one_group, jnp.zeros_like(psi_seg), inputs)
    return summed


def reference(psi, left_env, right_env, site_energy, mv_counts, mv_src, mv_dst, mv_coef,
              up_counts, up_block, up_top, up_bot, up_coef):
    residuals = []
    renewals = []
    quotients = []
    for segment in range(SEGS):
        renewal = renew_segment(psi[segment], left_env[segment], up_counts[segment], up_block[segment],
                                up_top[segment], up_bot[segment], up_coef[segment])
        renewals.append(renewal)
        env_used = left_env[0] if segment == 0 else renewals[segment - 1]
        applied = apply_segment(psi[segment], env_used, right_env[segment], mv_counts[segment],
                                mv_src[segment], mv_dst[segment], mv_coef[segment])
        applied = applied + site_energy[segment][:, None, None] * psi[segment]
        quotient = jnp.sum(psi[segment] * applied) / jnp.sum(psi[segment] * psi[segment])
        residuals.append(applied - quotient * psi[segment])
        quotients.append(quotient)
    return jnp.stack(residuals), jnp.stack(renewals), jnp.stack(quotients)
```

```python
import functools

import jax
import jax.numpy as jnp
from jax import lax
from jax.experimental import pallas as pl
from jax.experimental.pallas import tpu as pltpu
from jax.sharding import PartitionSpec as P

MAXT = 24
F32 = jnp.float32
BF16 = jnp.bfloat16
VMEM = pl.BlockSpec(memory_space=pltpu.VMEM)
SMEM = pl.BlockSpec(memory_space=pltpu.SMEM)
ANY = pl.BlockSpec(memory_space=pl.ANY)


def passed_along(value, axis, steps):
    count = lax.axis_size(axis)
    first, last = (max(0, -steps), min(count, count - steps))
    return lax.ppermute(value, axis, [(source, source + steps) for source in range(first, last)])


def slot_layout(counts, most):
    block_ends = jnp.cumsum(counts)
    block_starts = block_ends - counts
    slots = jnp.arange(most, dtype=jnp.int32)
    live_slot = slots[None, :] < counts[:, None]
    slot_pos = jnp.where(live_slot, block_starts[:, None] + slots[None, :], 0)
    return (slot_pos, live_slot)


def apply_terms(gathered, env_used, right_own, counts, sources, targets, coefs):
    psi_count = gathered.shape[0]
    tile_width = gathered.shape[1]
    channels = counts.shape[0]
    quarter = channels // 4
    slot_pos, live_slot = slot_layout(counts, MAXT)
    src_slots = sources[slot_pos]
    dst_slots = targets[slot_pos]
    coef_slots = jnp.where(live_slot, coefs[slot_pos], 0.0)

    def apply_one_turn(running, inputs):
        env_part, right_part, src_part, dst_part, coef_part = inputs
        inner = jnp.einsum(
            "csij,cjk->csik", gathered[src_part], right_part, precision=lax.Precision.HIGHEST
        )
        contrib = jnp.einsum("cij,csjk->csik", env_part, inner, precision=lax.Precision.HIGHEST)
        contrib = contrib * coef_part[:, :, None, None]
        added = jax.ops.segment_sum(
            contrib.reshape(-1, tile_width, tile_width),
            dst_part.reshape(-1),
            num_segments=psi_count,
        )
        return (running + added, None)

    inputs = (
        env_used.reshape(4, quarter, tile_width, tile_width),
        right_own.reshape(4, quarter, tile_width, tile_width),
        src_slots.reshape(4, quarter, MAXT),
        dst_slots.reshape(4, quarter, MAXT),
        coef_slots.reshape(4, quarter, MAXT),
    )
    start_sum = jnp.zeros((psi_count, tile_width, tile_width), jnp.float32)
    summed, unused = lax.scan(apply_one_turn, start_sum, inputs)
    return summed


def renew_env(gathered, own_env, counts, blocks, tops, bottoms, coefs):
    tile_width = gathered.shape[1]
    channels = counts.shape[0]
    quarter = channels // 4
    slot_pos, live_slot = slot_layout(counts, MAXT)
    block_slots = blocks[slot_pos]
    top_slots = tops[slot_pos]
    bottom_slots = bottoms[slot_pos]
    coef_slots = jnp.where(live_slot, coefs[slot_pos], 0.0)

    def renew_one_turn(inputs):
        block_part, top_part, bottom_part, coef_part = inputs
        inner = jnp.einsum(
            "csij,csjk->csik",
            own_env[block_part],
            gathered[bottom_part],
            precision=lax.Precision.HIGHEST,
        )
        contrib = jnp.einsum(
            "csji,csjk->csik", gathered[top_part], inner, precision=lax.Precision.HIGHEST
        )
        contrib = contrib * coef_part[:, :, None, None]
        return jnp.sum(contrib, axis=1)

    inputs = (
        block_slots.reshape(4, quarter, MAXT),
        top_slots.reshape(4, quarter, MAXT),
        bottom_slots.reshape(4, quarter, MAXT),
        coef_slots.reshape(4, quarter, MAXT),
    )
    stacked = lax.map(renew_one_turn, inputs)
    return stacked.reshape(channels, tile_width, tile_width)


def general_shards(
    psi,
    left_env,
    right_env,
    site_energy,
    mv_counts,
    mv_src,
    mv_dst,
    mv_coef,
    up_counts,
    up_block,
    up_top,
    up_bot,
    up_coef,
):
    own_psi = psi[0]
    own_env = left_env[0]
    gathered = lax.all_gather(own_psi, "tile", axis=0, tiled=True)
    renewal = renew_env(
        gathered,
        own_env,
        up_counts[0, 0],
        up_block[0, 0],
        up_top[0, 0],
        up_bot[0, 0],
        up_coef[0, 0],
    )
    received = passed_along(renewal, "seg", 1)
    leading = lax.axis_index("seg") == 0
    env_used = jnp.where(leading, own_env, received)
    partial_value = apply_terms(
        gathered, env_used, right_env[0], mv_counts[0, 0], mv_src[0, 0], mv_dst[0, 0], mv_coef[0, 0]
    )
    row_count = own_psi.shape[0]
    energies = site_energy[0]
    row_start = lax.axis_index("tile") * row_count
    summed_own = lax.psum_scatter(partial_value, "tile", scatter_dimension=0, tiled=True)
    own_energy = lax.dynamic_slice_in_dim(energies, row_start, row_count, 0)
    own_rows = summed_own + own_energy[:, None, None] * own_psi
    numerator = lax.psum(jnp.sum(own_psi * own_rows), "tile")
    denominator = jnp.sum(gathered * gathered)
    quotient = numerator / denominator
    residual = own_rows - quotient * own_psi
    return (residual[None], renewal[None], jnp.reshape(quotient, (1,)))


def heads_tails(value):
    head = value.astype(BF16)
    return head, (value - head.astype(F32)).astype(BF16)


def add_entries(total, entries, dst, src, coef, blocks):
    blocks[...] = jnp.zeros_like(blocks)

    def step(e, unused):
        target = dst[e]
        blocks[target] += coef[e] * entries[src[e]]
        return unused

    lax.fori_loop(0, total, step, 0, unroll=4)


def renew_kernel(*refs):
    n = len(refs) - 9
    dst, src, coef = refs[:3]
    tiles = refs[3 : 3 + n]
    env, out, bottoms, tops, entries, blocks = refs[3 + n : 9 + n]
    channels, w = env.shape[0], env.shape[1]
    for k in range(n):
        at = slice(k * w, (k + 1) * w)
        value = tiles[k][...]
        head, tail = heads_tails(value)
        bottoms[0:w, at] = head
        bottoms[w : 2 * w, at] = head
        bottoms[2 * w : 3 * w, at] = tail
        bottoms[3 * w : 4 * w, at] = tail
        head, tail = heads_tails(value.T)
        tops[0:w, at] = head
        tops[w : 2 * w, at] = tail
    group = channels // 2

    def products(g, unused):
        head, tail = heads_tails(env[pl.ds(g * group, group)].reshape(group * w, w))
        both = jnp.concatenate([head, tail, head, tail], axis=1)
        found = jnp.dot(both, bottoms[...], preferred_element_type=F32)
        for h in range(group):
            for k in range(n):
                entries[(g * group + h) * n + k] = found[h * w : (h + 1) * w, k * w : (k + 1) * w]
        return unused

    lax.fori_loop(0, 2, products, 0)
    add_entries(dst.shape[0], entries, dst, src, coef, blocks)

    def finish(b, unused):
        head, tail = heads_tails(blocks[pl.ds(b * n, n)].reshape(n * w, w))
        both = jnp.concatenate([head, tail], axis=1)
        found = jnp.dot(tops[...], both, preferred_element_type=F32)
        out[b] = (found[:w, :w] + found[w:, w:]) + (found[:w, w:] + found[w:, :w])
        return unused

    lax.fori_loop(0, channels, finish, 0, unroll=4)


def renew_call(dst, src, coef, tiles, env):
    n, w, channels = len(tiles), env.shape[1], env.shape[0]
    return pl.pallas_call(
        renew_kernel,
        out_shape=jax.ShapeDtypeStruct(env.shape, F32),
        in_specs=[SMEM] * 3 + [VMEM] * (n + 1),
        out_specs=VMEM,
        scratch_shapes=[
            pltpu.VMEM((4 * w, n * w), BF16),
            pltpu.VMEM((2 * w, n * w), BF16),
            pltpu.VMEM((channels * n, w, w), F32),
            pltpu.VMEM((channels * n, w, w), F32),
        ],
        compiler_params=pltpu.CompilerParams(vmem_limit_bytes=40 << 20),
        cost_estimate=pl.CostEstimate(flops=10**10, bytes_accessed=3 << 20, transcendentals=0),
        name="renew",
    )(dst, src, coef, *tiles, env)


def source_kernel(n, dst, src, coef, energies, *refs):
    tiles = refs[:n]
    right, out, stats, sources, entries, blocks = refs[n:]
    channels, w = right.shape[0], right.shape[1]
    weight = jnp.zeros((8, w), F32)
    energy = jnp.zeros((8, w), F32)
    for k in range(n):
        at = slice(k * w, (k + 1) * w)
        value = tiles[k][...]
        head, tail = heads_tails(value)
        sources[at, 0:w] = head
        sources[at, w : 2 * w] = tail
        sources[at, 2 * w : 3 * w] = head
        sources[at, 3 * w : 4 * w] = tail
        squares = jnp.sum((value * value).reshape(w // 8, 8, w), axis=0)
        weight += squares
        energy += energies[k] * squares
    stats[0:8] = weight
    stats[8:16] = energy

    def products(g, unused):
        columns = []
        for h in range(2):
            head, tail = heads_tails(right[2 * g + h])
            columns.append(jnp.concatenate([head, head, tail, tail], axis=0))
        found = jnp.dot(sources[...], jnp.concatenate(columns, axis=1), preferred_element_type=F32)
        for h in range(2):
            for k in range(n):
                entries[(2 * g + h) * n + k] = found[k * w : (k + 1) * w, h * w : (h + 1) * w]
        return unused

    lax.fori_loop(0, channels // 2, products, 0, unroll=2)
    add_entries(dst.shape[0], entries, dst, src, coef, blocks)

    def finish(c, unused):
        for k in range(n):
            head, tail = heads_tails(blocks[c * n + k])
            rows = pl.ds(pl.multiple_of(c * w, w), w)
            out[k, rows, 0:w] = head
            out[k, rows, w : 2 * w] = tail
        return unused

    lax.fori_loop(0, channels, finish, 0)


def source_call(dst, src, coef, energies, tiles, right):
    n, w, channels = len(tiles), right.shape[1], right.shape[0]
    return pl.pallas_call(
        functools.partial(source_kernel, n),
        out_shape=(
            jax.ShapeDtypeStruct((n, channels * w, 2 * w), BF16),
            jax.ShapeDtypeStruct((16, w), F32),
        ),
        in_specs=[SMEM] * 4 + [VMEM] * (n + 1),
        out_specs=(VMEM, VMEM),
        scratch_shapes=[
            pltpu.VMEM((n * w, 4 * w), BF16),
            pltpu.VMEM((channels * n, w, w), F32),
            pltpu.VMEM((channels * n, w, w), F32),
        ],
        compiler_params=pltpu.CompilerParams(vmem_limit_bytes=48 << 20),
        cost_estimate=pl.CostEstimate(flops=10**10, bytes_accessed=10 << 20, transcendentals=0),
        name="sources",
    )(dst, src, coef, energies, *tiles, right)


def apply_kernel(n, *refs):
    tiles = refs[:n]
    own, received, blocks = refs[n : n + 3]
    outs = refs[n + 3 : 2 * n + 3]
    env, lefts, arrived = refs[2 * n + 3 :]
    channels, w = env.shape[0], env.shape[1]
    leading = lax.axis_index("seg") == 0

    @pl.when(leading)
    def _():
        pltpu.make_async_copy(own, env, arrived).start()

    @pl.when(jnp.logical_not(leading))
    def _():
        pltpu.make_async_copy(received, env, arrived).start()

    pltpu.make_async_copy(own, env, arrived).wait()
    for c in range(channels):
        head, tail = heads_tails(env[c])
        lefts[0:w, c * w : (c + 1) * w] = head
        lefts[w : 2 * w, c * w : (c + 1) * w] = tail
    inner = jnp.zeros((8, w), F32)
    for k in range(n):
        found = jnp.dot(lefts[...], blocks[k], preferred_element_type=F32)
        value = (found[:w, :w] + found[w:, w:]) + (found[:w, w:] + found[w:, :w])
        outs[k][0:w] = value
        inner += jnp.sum((value * tiles[k][...]).reshape(w // 8, 8, w), axis=0)
    for k in range(n):
        outs[k][w : w + 8] = inner


def apply_call(tiles, own, received, blocks):
    n, w = len(tiles), own.shape[1]
    return pl.pallas_call(
        functools.partial(apply_kernel, n),
        out_shape=tuple(jax.ShapeDtypeStruct((w + 8, w), F32) for _ in range(n)),
        in_specs=[VMEM] * n + [ANY, ANY, VMEM],
        out_specs=(VMEM,) * n,
        scratch_shapes=[
            pltpu.VMEM(own.shape, F32),
            pltpu.VMEM((2 * w, own.shape[0] * w), BF16),
            pltpu.SemaphoreType.DMA,
        ],
        compiler_params=pltpu.CompilerParams(vmem_limit_bytes=32 << 20),
        cost_estimate=pl.CostEstimate(flops=5 * 10**9, bytes_accessed=10 << 20, transcendentals=0),
        name="applied",
    )(*tiles, own, received, blocks)


def finish_kernel(energy, *refs):
    parts = refs[:-4]
    own, stats, residual, quotient = refs[-4:]
    w = own.shape[0]
    total = parts[0][...]
    for part in parts[1:]:
        total = total + part[...]
    value = own[...]
    numerator = jnp.sum(total[w : w + 8]) + jnp.sum(stats[8:16])
    ratio = jnp.full((1, 128), numerator, F32) / jnp.full((1, 128), jnp.sum(stats[0:8]), F32)
    residual[...] = total[:w] + (energy[0] - ratio) * value
    quotient[...] = ratio


def finish_call(energy, parts, own, stats):
    w = own.shape[0]
    return pl.pallas_call(
        finish_kernel,
        out_shape=(jax.ShapeDtypeStruct((w, w), F32), jax.ShapeDtypeStruct((1, 128), F32)),
        in_specs=[SMEM] + [VMEM] * (len(parts) + 2),
        out_specs=(VMEM, VMEM),
        name="finish",
    )(energy, *parts, own, stats)


def channel_of(counts, live):
    ends = jnp.cumsum(counts)
    return jnp.sum((jnp.arange(live)[:, None] >= ends[None, :]).astype(jnp.int32), axis=1)


def shards(
    psi,
    left_env,
    right_env,
    site_energy,
    mv_counts,
    mv_src,
    mv_dst,
    mv_coef,
    up_counts,
    up_block,
    up_top,
    up_bot,
    up_coef,
):
    n = lax.axis_size("tile")
    me = lax.axis_index("tile")
    live = mv_src.shape[2]

    def across(value, k):
        return lax.ppermute(value, "tile", [(i, i ^ k) for i in range(n)])

    own = psi[0, 0]
    tiles = {0: own, 1: across(own, 1)}
    for k in range(n - 2, 0, -2):
        tiles[k] = across(own, k)
    for k in range(2, n, 2):
        tiles[k + 1] = across(tiles[k], 1)
    tiles = [tiles[k] for k in range(n)]

    up_channel = channel_of(up_counts[0, 0], live)
    up_dst = up_channel * n + (up_top[0, 0] ^ me)
    up_from = up_block[0, 0] * n + (up_bot[0, 0] ^ me)
    mv_channel = channel_of(mv_counts[0, 0], live)
    mv_to = mv_channel * n + (mv_dst[0, 0] ^ me)
    mv_from = mv_channel * n + (mv_src[0, 0] ^ me)
    energies = site_energy[0][jnp.arange(n) ^ me]

    renewal = renew_call(up_dst, up_from, up_coef[0, 0], tiles, left_env[0])
    received = passed_along(renewal, "seg", 1)
    blocks, stats = source_call(mv_to, mv_from, mv_coef[0, 0], energies, tiles, right_env[0])
    partials = apply_call(tiles, left_env[0], received, blocks)

    parts = [partials[0]]
    for k in range(n - 2, 0, -2):
        parts.append(across(partials[k] + across(partials[k + 1], 1), k))
    parts.append(across(partials[1], 1))
    residual, quotient = finish_call(energies, parts, own, stats)
    return (residual[None, None], renewal[None], quotient[0, :1])


def solution(mesh):
    per_run = P(("parts", "seg"), "tile", None)
    return jax.shard_map(
        shards if mesh.shape["tile"] == 8 else general_shards,
        mesh=mesh,
        in_specs=(
            P(("parts", "seg"), "tile", None, None),
            P(("parts", "seg"), "tile", None, None),
            P(("parts", "seg"), "tile", None, None),
            P(("parts", "seg"), None),
            per_run,
            per_run,
            per_run,
            per_run,
            per_run,
            per_run,
            per_run,
            per_run,
            per_run,
        ),
        out_specs=(
            P(("parts", "seg"), "tile", None, None),
            P(("parts", "seg"), "tile", None, None),
            P(("parts", "seg")),
        ),
        check_vma=False,
    )
```

```python
import functools

import jax
import jax.numpy as jnp
from jax import lax
from jax.experimental import pallas as pl
from jax.experimental.pallas import tpu as pltpu
from jax.sharding import PartitionSpec as P

MAXT = 24
F32 = jnp.float32
BF16 = jnp.bfloat16
VMEM = pl.BlockSpec(memory_space=pltpu.VMEM)
SMEM = pl.BlockSpec(memory_space=pltpu.SMEM)
ANY = pl.BlockSpec(memory_space=pl.ANY)
HBM = pl.BlockSpec(memory_space=pltpu.HBM)


def passed_along(value, axis, steps):
    count = lax.axis_size(axis)
    first, last = (max(0, -steps), min(count, count - steps))
    return lax.ppermute(value, axis, [(source, source + steps) for source in range(first, last)])


def slot_layout(counts, most):
    block_ends = jnp.cumsum(counts)
    block_starts = block_ends - counts
    slots = jnp.arange(most, dtype=jnp.int32)
    live_slot = slots[None, :] < counts[:, None]
    slot_pos = jnp.where(live_slot, block_starts[:, None] + slots[None, :], 0)
    return (slot_pos, live_slot)


def apply_terms(gathered, env_used, right_own, counts, sources, targets, coefs):
    psi_count = gathered.shape[0]
    tile_width = gathered.shape[1]
    channels = counts.shape[0]
    quarter = channels // 4
    slot_pos, live_slot = slot_layout(counts, MAXT)
    src_slots = sources[slot_pos]
    dst_slots = targets[slot_pos]
    coef_slots = jnp.where(live_slot, coefs[slot_pos], 0.0)

    def apply_one_turn(running, inputs):
        env_part, right_part, src_part, dst_part, coef_part = inputs
        inner = jnp.einsum(
            "csij,cjk->csik", gathered[src_part], right_part, precision=lax.Precision.HIGHEST
        )
        contrib = jnp.einsum("cij,csjk->csik", env_part, inner, precision=lax.Precision.HIGHEST)
        contrib = contrib * coef_part[:, :, None, None]
        added = jax.ops.segment_sum(
            contrib.reshape(-1, tile_width, tile_width),
            dst_part.reshape(-1),
            num_segments=psi_count,
        )
        return (running + added, None)

    inputs = (
        env_used.reshape(4, quarter, tile_width, tile_width),
        right_own.reshape(4, quarter, tile_width, tile_width),
        src_slots.reshape(4, quarter, MAXT),
        dst_slots.reshape(4, quarter, MAXT),
        coef_slots.reshape(4, quarter, MAXT),
    )
    start_sum = jnp.zeros((psi_count, tile_width, tile_width), jnp.float32)
    summed, unused = lax.scan(apply_one_turn, start_sum, inputs)
    return summed


def renew_env(gathered, own_env, counts, blocks, tops, bottoms, coefs):
    tile_width = gathered.shape[1]
    channels = counts.shape[0]
    quarter = channels // 4
    slot_pos, live_slot = slot_layout(counts, MAXT)
    block_slots = blocks[slot_pos]
    top_slots = tops[slot_pos]
    bottom_slots = bottoms[slot_pos]
    coef_slots = jnp.where(live_slot, coefs[slot_pos], 0.0)

    def renew_one_turn(inputs):
        block_part, top_part, bottom_part, coef_part = inputs
        inner = jnp.einsum(
            "csij,csjk->csik",
            own_env[block_part],
            gathered[bottom_part],
            precision=lax.Precision.HIGHEST,
        )
        contrib = jnp.einsum(
            "csji,csjk->csik", gathered[top_part], inner, precision=lax.Precision.HIGHEST
        )
        contrib = contrib * coef_part[:, :, None, None]
        return jnp.sum(contrib, axis=1)

    inputs = (
        block_slots.reshape(4, quarter, MAXT),
        top_slots.reshape(4, quarter, MAXT),
        bottom_slots.reshape(4, quarter, MAXT),
        coef_slots.reshape(4, quarter, MAXT),
    )
    stacked = lax.map(renew_one_turn, inputs)
    return stacked.reshape(channels, tile_width, tile_width)


def general_shards(
    psi,
    left_env,
    right_env,
    site_energy,
    mv_counts,
    mv_src,
    mv_dst,
    mv_coef,
    up_counts,
    up_block,
    up_top,
    up_bot,
    up_coef,
):
    own_psi = psi[0]
    own_env = left_env[0]
    gathered = lax.all_gather(own_psi, "tile", axis=0, tiled=True)
    renewal = renew_env(
        gathered,
        own_env,
        up_counts[0, 0],
        up_block[0, 0],
        up_top[0, 0],
        up_bot[0, 0],
        up_coef[0, 0],
    )
    received = passed_along(renewal, "seg", 1)
    leading = lax.axis_index("seg") == 0
    env_used = jnp.where(leading, own_env, received)
    partial_value = apply_terms(
        gathered, env_used, right_env[0], mv_counts[0, 0], mv_src[0, 0], mv_dst[0, 0], mv_coef[0, 0]
    )
    row_count = own_psi.shape[0]
    energies = site_energy[0]
    row_start = lax.axis_index("tile") * row_count
    summed_own = lax.psum_scatter(partial_value, "tile", scatter_dimension=0, tiled=True)
    own_energy = lax.dynamic_slice_in_dim(energies, row_start, row_count, 0)
    own_rows = summed_own + own_energy[:, None, None] * own_psi
    numerator = lax.psum(jnp.sum(own_psi * own_rows), "tile")
    denominator = jnp.sum(gathered * gathered)
    quotient = numerator / denominator
    residual = own_rows - quotient * own_psi
    return (residual[None], renewal[None], jnp.reshape(quotient, (1,)))


def heads_tails(value):
    head = value.astype(BF16)
    return head, (value - head.astype(F32)).astype(BF16)


def side_by_side(value):
    return jnp.concatenate(heads_tails(value), axis=1)


def product(left, right):
    return jnp.dot(left, right, preferred_element_type=F32)


def channel_row(counts, live, channels):
    at = lax.broadcasted_iota(jnp.int32, (1, live), 1)
    found = jnp.zeros((1, live), jnp.int32)
    end = 0
    for c in range(channels):
        end = end + counts[0, 0, c]
        found += (at >= end).astype(jnp.int32)
    return found


def thirds(value):
    first = value.astype(BF16)
    value = value - first.astype(F32)
    second = value.astype(BF16)
    return [first.astype(F32), second.astype(F32), value - second.astype(F32)]


def over_entries(rows, chosen):
    return lax.dot_general(
        rows.astype(BF16), chosen, (((1,), (1,)), ((), ())), preferred_element_type=F32
    )


def plan_terms(group, source, coef, ints, floats):
    w, live = 128, group.shape[1]
    groups = lax.broadcasted_iota(jnp.int32, (w, live), 0)
    member = group == groups
    ones = jnp.where(member, 1.0, 0.0)
    earlier = lax.broadcasted_iota(jnp.int32, (live, live), 0) < lax.broadcasted_iota(
        jnp.int32, (live, live), 1
    )
    earlier = jnp.where(earlier, 1.0, 0.0).astype(BF16)
    before = product(ones.astype(BF16), earlier)
    size = jnp.sum(ones, axis=1, keepdims=True)
    rank = jnp.sum(ones * before, axis=0, keepdims=True)
    size_here = jnp.sum(ones * size, axis=0, keepdims=True)
    spilled = jnp.where(size_here > 2.0, jnp.where(rank > 0.0, 1.0, 0.0), 0.0)
    parts = thirds(coef)
    sources = source.astype(F32)
    zero = jnp.zeros_like(coef)
    rows = jnp.concatenate([sources, *parts, ones[0:1] * 0.0 + 1.0, zero, zero, zero], axis=0)
    first = over_entries(rows, jnp.where(before == 0.0, ones, 0.0).astype(BF16))
    second = over_entries(rows, jnp.where(before == 1.0, ones, 0.0).astype(BF16))
    large = over_entries(rows, ones.astype(BF16))[4:5] > 2.0
    at = lax.broadcasted_iota(jnp.int32, (1, w), 1)
    ints[0:1, 0:w] = first[0:1].astype(jnp.int32)
    ints[1:2, 0:w] = jnp.where(large, w + at, second[0:1].astype(jnp.int32))
    floats[0:1, 0:w] = first[1:2] + first[2:3] + first[3:4]
    floats[1:2, 0:w] = jnp.where(large, 1.0, second[1:2] + second[2:3] + second[3:4])

    place = product(jnp.concatenate([spilled] * 8, axis=0).astype(BF16), earlier)[0:1]
    place = jnp.where(spilled > 0.0, place, -1.0)
    column = lax.broadcasted_iota(jnp.int32, (live, live), 0).astype(F32)
    chosen = jnp.where(place == column, 1.0, 0.0).astype(BF16)
    again = jnp.where(rank > 1.0, 1.0, 0.0)
    rows = jnp.concatenate(
        [sources, *parts, (group + w).astype(F32), again, zero, zero], axis=0
    )
    listed = over_entries(rows, chosen)
    ints[2:3] = listed[0:1].astype(jnp.int32)
    ints[3:4] = listed[4:5].astype(jnp.int32)
    ints[4:5] = jnp.full((1, live), jnp.sum(spilled)).astype(jnp.int32)
    floats[2:3] = listed[1:2] + listed[2:3] + listed[3:4]
    floats[3:4] = listed[5:6]


def spill(ints, floats, blocks):
    def add(q, unused):
        to = ints[3, q]
        held = jnp.where(floats[3, q] > 0.0, blocks[to], 0.0)
        blocks[to] = held + floats[2, q] * blocks[ints[2, q]]
        return unused

    lax.fori_loop(0, ints[4, 0], add, 0)


def two_terms(ints, floats, blocks, g):
    return floats[0, g] * blocks[ints[0, g]] + floats[1, g] * blocks[ints[1, g]]


def prepare_kernel(n, *refs):
    psi, given, refs = refs[0], refs[1:12], refs[12:]
    lefts, rights, up_ints, up_floats, mv_ints, mv_floats, own = refs[:7]
    held = refs[7:18]
    arrived, own_arrived = refs[18:]
    own_copy = pltpu.make_async_copy(psi.at[0, 0], own, own_arrived)
    own_copy.start()
    copies = [
        pltpu.make_async_copy(source, target, arrived.at[index])
        for index, (source, target) in enumerate(zip(given, held))
    ]
    for copy in copies:
        copy.start()
    up_counts, up_block, up_top, up_bot, up_coef, mv_counts, mv_src, mv_dst, mv_coef = held[:9]
    left, right = held[9:]
    channels, w = left.shape[1], left.shape[2]
    live = up_block.shape[2]
    me = lax.axis_index("tile")
    for copy in copies[:9]:
        copy.wait()
    channel = channel_row(up_counts, live, channels)
    plan_terms(
        channel * n + (up_top[0] ^ me), up_block[0] * n + (up_bot[0] ^ me), up_coef[0], up_ints, up_floats
    )
    channel = channel_row(mv_counts, live, channels)
    plan_terms(
        channel * n + (mv_dst[0] ^ me), channel * n + (mv_src[0] ^ me), mv_coef[0], mv_ints, mv_floats
    )
    copies[9].wait()

    def halve_left(c, unused):
        lefts[pl.ds(pl.multiple_of(c * w, w), w)] = side_by_side(left[0, c])
        return unused

    lax.fori_loop(0, channels, halve_left, 0, unroll=2)
    copies[10].wait()

    def halve_right(c, unused):
        head, tail = heads_tails(right[0, c])
        rights[c, 0:w] = head
        rights[c, w : 2 * w] = tail
        return unused

    lax.fori_loop(0, channels, halve_right, 0, unroll=2)
    own_copy.wait()


def prepare_call(n, psi, given):
    channels, w = given[-1].shape[1], given[-1].shape[2]
    live = given[1].shape[2]
    table = (8, live)
    return pl.pallas_call(
        functools.partial(prepare_kernel, n),
        out_shape=(
            jax.ShapeDtypeStruct((channels * w, 2 * w), BF16),
            jax.ShapeDtypeStruct((channels, 2 * w, w), BF16),
            jax.ShapeDtypeStruct(table, jnp.int32),
            jax.ShapeDtypeStruct(table, F32),
            jax.ShapeDtypeStruct(table, jnp.int32),
            jax.ShapeDtypeStruct(table, F32),
            jax.ShapeDtypeStruct((w, w), F32),
        ),
        in_specs=[HBM] * (len(given) + 1),
        out_specs=(VMEM,) * 7,
        scratch_shapes=[
            *(
                pltpu.SMEM(x.shape, x.dtype) if x.shape[-1] == channels else pltpu.VMEM(x.shape, x.dtype)
                for x in given
            ),
            pltpu.SemaphoreType.DMA((len(given),)),
            pltpu.SemaphoreType.DMA,
        ],
        compiler_params=pltpu.CompilerParams(vmem_limit_bytes=12 << 20),
        cost_estimate=pl.CostEstimate(flops=10**9, bytes_accessed=6 << 20, transcendentals=0),
        name="prepare",
    )(*(pltpu.with_memory_space_constraint(x, pltpu.HBM) for x in (psi, *given)))


def fetch_tables(sources, targets, arrived):
    copies = [
        pltpu.make_async_copy(source, target, arrived.at[index])
        for index, (source, target) in enumerate(zip(sources, targets))
    ]
    for copy in copies:
        copy.start()
    return copies


def renew_kernel(n, *refs):
    tiles = refs[:n]
    lefts, int_table, float_table, out, bottoms, tops, entries, renewed, ints, floats, arrived, left = refs[n:]
    channels, w = out.shape[0], out.shape[1]
    copies = fetch_tables((int_table, float_table), (ints, floats), arrived)
    for k in range(n):
        at = slice(k * w, (k + 1) * w)
        value = tiles[k][...]
        head, tail = heads_tails(value)
        bottoms[0:w, at] = head
        bottoms[w : 2 * w, at] = head
        bottoms[2 * w : 3 * w, at] = tail
        bottoms[3 * w : 4 * w, at] = tail
        head, tail = heads_tails(value.T)
        tops[0:w, at] = head
        tops[w : 2 * w, at] = tail
    group = channels // 2

    def multiply(g, unused):
        own = lefts[pl.ds(pl.multiple_of(g * (group * w), group * w), group * w)]
        found = product(jnp.concatenate([own, own], axis=1), bottoms[...])
        for h in range(group):
            for k in range(n):
                entries[(g * group + h) * n + k] = found[h * w : (h + 1) * w, k * w : (k + 1) * w]
        return unused

    lax.fori_loop(0, 2, multiply, 0)
    for copy in copies:
        copy.wait()
    spill(ints, floats, entries)

    def finish(b, unused):
        pairs = [heads_tails(two_terms(ints, floats, entries, b * n + k)) for k in range(n)]
        stack = [jnp.concatenate([pair[i] for pair in pairs], axis=0) for i in range(2)]
        found = product(tops[...], jnp.concatenate(stack, axis=1))
        renewed[b] = (found[:w, :w] + found[w:, w:]) + (found[:w, w:] + found[w:, :w])
        pltpu.make_async_copy(renewed.at[b], out.at[b], left.at[b]).start()
        return unused

    lax.fori_loop(0, channels, finish, 0, unroll=8)
    for b in range(channels):
        pltpu.make_async_copy(renewed.at[b], out.at[b], left.at[b]).wait()


def renew_call(tiles, lefts, int_table, float_table, channels):
    n, w = len(tiles), tiles[0].shape[0]
    return pl.pallas_call(
        functools.partial(renew_kernel, n),
        out_shape=jax.ShapeDtypeStruct((channels, w, w), F32),
        in_specs=[VMEM] * (n + 1) + [ANY] * 2,
        out_specs=HBM,
        scratch_shapes=[
            pltpu.VMEM((4 * w, n * w), BF16),
            pltpu.VMEM((2 * w, n * w), BF16),
            pltpu.VMEM((2 * w, w, w), F32),
            pltpu.VMEM((channels, w, w), F32),
            pltpu.SMEM(int_table.shape, jnp.int32),
            pltpu.SMEM(float_table.shape, F32),
            pltpu.SemaphoreType.DMA((2,)),
            pltpu.SemaphoreType.DMA((channels,)),
        ],
        compiler_params=pltpu.CompilerParams(vmem_limit_bytes=28 << 20),
        cost_estimate=pl.CostEstimate(flops=10**10, bytes_accessed=3 << 20, transcendentals=0),
        name="renew",
    )(*tiles, lefts, int_table, float_table)


def source_kernel(n, energies, *refs):
    tiles = refs[:n]
    rights, int_table, float_table, out, stats, sources, entries, ints, floats, arrived = refs[n:]
    channels, w = rights.shape[0], rights.shape[2]
    copies = fetch_tables((int_table, float_table), (ints, floats), arrived)
    me = lax.axis_index("tile")
    weight = jnp.zeros((8, w), F32)
    energy = jnp.zeros((8, w), F32)
    for k in range(n):
        at = slice(k * w, (k + 1) * w)
        value = tiles[k][...]
        head, tail = heads_tails(value)
        sources[at, 0:w] = head
        sources[at, w : 2 * w] = tail
        sources[at, 2 * w : 3 * w] = head
        sources[at, 3 * w : 4 * w] = tail
        squares = jnp.sum((value * value).reshape(w // 8, 8, w), axis=0)
        weight += squares
        energy += energies[0, k ^ me] * squares
    stats[0:8] = weight
    stats[8:16] = energy
    stats[16:24] = jnp.full((8, w), energies[0, me], F32)
    group = channels // 2

    def multiply(g, unused):
        columns = []
        for h in range(group):
            value = rights[g * group + h]
            columns.append(jnp.concatenate([value[:w], value[:w], value[w:], value[w:]], axis=0))
        found = product(sources[...], jnp.concatenate(columns, axis=1))
        for h in range(group):
            for k in range(n):
                entries[(g * group + h) * n + k] = found[k * w : (k + 1) * w, h * w : (h + 1) * w]
        return unused

    lax.fori_loop(0, 2, multiply, 0)
    for copy in copies:
        copy.wait()
    spill(ints, floats, entries)

    def finish(c, unused):
        rows = pl.ds(pl.multiple_of(c * w, w), w)
        for k in range(n):
            out[k, rows] = side_by_side(two_terms(ints, floats, entries, c * n + k))
        return unused

    lax.fori_loop(0, channels, finish, 0, unroll=2)


def source_call(energies, tiles, rights, int_table, float_table):
    n, w, channels = len(tiles), rights.shape[2], rights.shape[0]
    return pl.pallas_call(
        functools.partial(source_kernel, n),
        out_shape=(
            jax.ShapeDtypeStruct((n, channels * w, 2 * w), BF16),
            jax.ShapeDtypeStruct((24, w), F32),
        ),
        in_specs=[SMEM] + [VMEM] * (n + 1) + [ANY] * 2,
        out_specs=(VMEM, VMEM),
        scratch_shapes=[
            pltpu.VMEM((n * w, 4 * w), BF16),
            pltpu.VMEM((2 * w, w, w), F32),
            pltpu.SMEM(int_table.shape, jnp.int32),
            pltpu.SMEM(float_table.shape, F32),
            pltpu.SemaphoreType.DMA((2,)),
        ],
        compiler_params=pltpu.CompilerParams(vmem_limit_bytes=28 << 20),
        cost_estimate=pl.CostEstimate(flops=10**10, bytes_accessed=10 << 20, transcendentals=0),
        name="sources",
    )(energies, *tiles, rights, int_table, float_table)


def apply_kernel(n, *refs):
    tiles = refs[:n]
    own, received, blocks = refs[n : n + 3]
    outs = refs[n + 3 : 2 * n + 3]
    env, lefts, arrived = refs[2 * n + 3 :]
    channels, w = env.shape[0], env.shape[1]
    leading = lax.axis_index("seg") == 0

    @pl.when(leading)
    def _():
        pltpu.make_async_copy(own, env, arrived).start()

    @pl.when(jnp.logical_not(leading))
    def _():
        pltpu.make_async_copy(received, env, arrived).start()

    pltpu.make_async_copy(own, env, arrived).wait()
    for c in range(channels):
        head, tail = heads_tails(env[c])
        lefts[0:w, c * w : (c + 1) * w] = head
        lefts[w : 2 * w, c * w : (c + 1) * w] = tail
    inner = jnp.zeros((8, w), F32)
    for k in range(n):
        found = jnp.dot(lefts[...], blocks[k], preferred_element_type=F32)
        value = (found[:w, :w] + found[w:, w:]) + (found[:w, w:] + found[w:, :w])
        outs[k][0:w] = value
        inner += jnp.sum((value * tiles[k][...]).reshape(w // 8, 8, w), axis=0)
    for k in range(n):
        outs[k][w : w + 8] = inner


def apply_call(tiles, own, received, blocks):
    n, w = len(tiles), own.shape[1]
    return pl.pallas_call(
        functools.partial(apply_kernel, n),
        out_shape=tuple(jax.ShapeDtypeStruct((w + 8, w), F32) for _ in range(n)),
        in_specs=[VMEM] * n + [ANY, ANY, VMEM],
        out_specs=(VMEM,) * n,
        scratch_shapes=[
            pltpu.VMEM(own.shape, F32),
            pltpu.VMEM((2 * w, own.shape[0] * w), BF16),
            pltpu.SemaphoreType.DMA,
        ],
        compiler_params=pltpu.CompilerParams(vmem_limit_bytes=8 << 20),
        cost_estimate=pl.CostEstimate(flops=5 * 10**9, bytes_accessed=10 << 20, transcendentals=0),
        name="applied",
    )(*tiles, own, received, blocks)


def finish_kernel(*refs):
    parts = refs[:-4]
    own, stats, residual, quotient = refs[-4:]
    w = own.shape[0]
    total = parts[0][...]
    for part in parts[1:]:
        total = total + part[...]
    value = own[...]
    numerator = jnp.sum(total[w : w + 8]) + jnp.sum(stats[8:16])
    ratio = jnp.full((1, 128), numerator, F32) / jnp.full((1, 128), jnp.sum(stats[0:8]), F32)
    residual[...] = total[:w] + (stats[16:17] - ratio) * value
    quotient[...] = ratio


def finish_call(parts, own, stats):
    w = own.shape[0]
    return pl.pallas_call(
        finish_kernel,
        out_shape=(jax.ShapeDtypeStruct((w, w), F32), jax.ShapeDtypeStruct((1, 128), F32)),
        in_specs=[VMEM] * (len(parts) + 2),
        out_specs=(VMEM, VMEM),
        compiler_params=pltpu.CompilerParams(vmem_limit_bytes=2 << 20),
        name="finish",
    )(*parts, own, stats)


def shards(
    psi,
    left_env,
    right_env,
    site_energy,
    mv_counts,
    mv_src,
    mv_dst,
    mv_coef,
    up_counts,
    up_block,
    up_top,
    up_bot,
    up_coef,
):
    n = lax.axis_size("tile")
    def across(value, k):
        return lax.ppermute(value, "tile", [(i, i ^ k) for i in range(n)])

    own = psi[0, 0]
    tiles = {0: own, 1: across(own, 1)}
    for k in range(n - 2, 0, -2):
        tiles[k] = across(own, k)
    for k in range(2, n, 2):
        tiles[k + 1] = across(tiles[k], 1)
    tiles = [tiles[k] for k in range(n)]

    given = [up_counts, up_block, up_top, up_bot, up_coef, mv_counts, mv_src, mv_dst, mv_coef]
    lefts, rights, up_ints, up_floats, mv_ints, mv_floats, own = prepare_call(
        n, psi, [*given, left_env, right_env]
    )
    tiles[0] = own
    renewal = renew_call(tiles, lefts, up_ints, up_floats, left_env.shape[1])
    received = passed_along(renewal, "seg", 1)
    blocks, stats = source_call(site_energy, tiles, rights, mv_ints, mv_floats)
    partials = apply_call(tiles, left_env[0], received, blocks)

    parts = [partials[0]]
    for k in range(n - 2, 0, -2):
        parts.append(across(partials[k] + across(partials[k + 1], 1), k))
    parts.append(across(partials[1], 1))
    residual, quotient = finish_call(parts, own, stats)
    return (residual[None, None], renewal[None], quotient[0, :1])


def solution(mesh):
    per_run = P(("parts", "seg"), "tile", None)
    return jax.shard_map(
        shards if mesh.shape["tile"] == 8 else general_shards,
        mesh=mesh,
        in_specs=(
            P(("parts", "seg"), "tile", None, None),
            P(("parts", "seg"), "tile", None, None),
            P(("parts", "seg"), "tile", None, None),
            P(("parts", "seg"), None),
            per_run,
            per_run,
            per_run,
            per_run,
            per_run,
            per_run,
            per_run,
            per_run,
            per_run,
        ),
        out_specs=(
            P(("parts", "seg"), "tile", None, None),
            P(("parts", "seg"), "tile", None, None),
            P(("parts", "seg")),
        ),
        check_vma=False,
    )
```

```python
import functools

import jax
import jax.numpy as jnp
from jax import lax
from jax.experimental import pallas as pl
from jax.experimental.pallas import tpu as pltpu
from jax.sharding import PartitionSpec as P

MAXT = 24
ORDER = (0, 1, 4, 2, 6, 5, 3, 7)
F32 = jnp.float32
BF16 = jnp.bfloat16
VMEM = pl.BlockSpec(memory_space=pltpu.VMEM)
SMEM = pl.BlockSpec(memory_space=pltpu.SMEM)
ANY = pl.BlockSpec(memory_space=pl.ANY)
HBM = pl.BlockSpec(memory_space=pltpu.HBM)


def passed_along(value, axis, steps):
    count = lax.axis_size(axis)
    first, last = (max(0, -steps), min(count, count - steps))
    return lax.ppermute(value, axis, [(source, source + steps) for source in range(first, last)])


def slot_layout(counts, most):
    block_ends = jnp.cumsum(counts)
    block_starts = block_ends - counts
    slots = jnp.arange(most, dtype=jnp.int32)
    live_slot = slots[None, :] < counts[:, None]
    slot_pos = jnp.where(live_slot, block_starts[:, None] + slots[None, :], 0)
    return (slot_pos, live_slot)


def apply_terms(gathered, env_used, right_own, counts, sources, targets, coefs):
    psi_count = gathered.shape[0]
    tile_width = gathered.shape[1]
    channels = counts.shape[0]
    quarter = channels // 4
    slot_pos, live_slot = slot_layout(counts, MAXT)
    src_slots = sources[slot_pos]
    dst_slots = targets[slot_pos]
    coef_slots = jnp.where(live_slot, coefs[slot_pos], 0.0)

    def apply_one_turn(running, inputs):
        env_part, right_part, src_part, dst_part, coef_part = inputs
        inner = jnp.einsum(
            "csij,cjk->csik", gathered[src_part], right_part, precision=lax.Precision.HIGHEST
        )
        contrib = jnp.einsum("cij,csjk->csik", env_part, inner, precision=lax.Precision.HIGHEST)
        contrib = contrib * coef_part[:, :, None, None]
        added = jax.ops.segment_sum(
            contrib.reshape(-1, tile_width, tile_width),
            dst_part.reshape(-1),
            num_segments=psi_count,
        )
        return (running + added, None)

    inputs = (
        env_used.reshape(4, quarter, tile_width, tile_width),
        right_own.reshape(4, quarter, tile_width, tile_width),
        src_slots.reshape(4, quarter, MAXT),
        dst_slots.reshape(4, quarter, MAXT),
        coef_slots.reshape(4, quarter, MAXT),
    )
    start_sum = jnp.zeros((psi_count, tile_width, tile_width), jnp.float32)
    summed, unused = lax.scan(apply_one_turn, start_sum, inputs)
    return summed


def renew_env(gathered, own_env, counts, blocks, tops, bottoms, coefs):
    tile_width = gathered.shape[1]
    channels = counts.shape[0]
    quarter = channels // 4
    slot_pos, live_slot = slot_layout(counts, MAXT)
    block_slots = blocks[slot_pos]
    top_slots = tops[slot_pos]
    bottom_slots = bottoms[slot_pos]
    coef_slots = jnp.where(live_slot, coefs[slot_pos], 0.0)

    def renew_one_turn(inputs):
        block_part, top_part, bottom_part, coef_part = inputs
        inner = jnp.einsum(
            "csij,csjk->csik",
            own_env[block_part],
            gathered[bottom_part],
            precision=lax.Precision.HIGHEST,
        )
        contrib = jnp.einsum(
            "csji,csjk->csik", gathered[top_part], inner, precision=lax.Precision.HIGHEST
        )
        contrib = contrib * coef_part[:, :, None, None]
        return jnp.sum(contrib, axis=1)

    inputs = (
        block_slots.reshape(4, quarter, MAXT),
        top_slots.reshape(4, quarter, MAXT),
        bottom_slots.reshape(4, quarter, MAXT),
        coef_slots.reshape(4, quarter, MAXT),
    )
    stacked = lax.map(renew_one_turn, inputs)
    return stacked.reshape(channels, tile_width, tile_width)


def general_shards(
    psi,
    left_env,
    right_env,
    site_energy,
    mv_counts,
    mv_src,
    mv_dst,
    mv_coef,
    up_counts,
    up_block,
    up_top,
    up_bot,
    up_coef,
):
    own_psi = psi[0]
    own_env = left_env[0]
    gathered = lax.all_gather(own_psi, "tile", axis=0, tiled=True)
    renewal = renew_env(
        gathered,
        own_env,
        up_counts[0, 0],
        up_block[0, 0],
        up_top[0, 0],
        up_bot[0, 0],
        up_coef[0, 0],
    )
    received = passed_along(renewal, "seg", 1)
    leading = lax.axis_index("seg") == 0
    env_used = jnp.where(leading, own_env, received)
    partial_value = apply_terms(
        gathered, env_used, right_env[0], mv_counts[0, 0], mv_src[0, 0], mv_dst[0, 0], mv_coef[0, 0]
    )
    row_count = own_psi.shape[0]
    energies = site_energy[0]
    row_start = lax.axis_index("tile") * row_count
    summed_own = lax.psum_scatter(partial_value, "tile", scatter_dimension=0, tiled=True)
    own_energy = lax.dynamic_slice_in_dim(energies, row_start, row_count, 0)
    own_rows = summed_own + own_energy[:, None, None] * own_psi
    numerator = lax.psum(jnp.sum(own_psi * own_rows), "tile")
    denominator = jnp.sum(gathered * gathered)
    quotient = numerator / denominator
    residual = own_rows - quotient * own_psi
    return (residual[None], renewal[None], jnp.reshape(quotient, (1,)))


def heads_tails(value):
    head = value.astype(BF16)
    return head, (value - head.astype(F32)).astype(BF16)


def side_by_side(value):
    return jnp.concatenate(heads_tails(value), axis=1)


def product(left, right):
    return jnp.dot(left, right, preferred_element_type=F32)


def channel_row(counts, live, channels):
    at = lax.broadcasted_iota(jnp.int32, (1, live), 1)
    found = jnp.zeros((1, live), jnp.int32)
    end = 0
    for c in range(channels):
        end = end + counts[0, 0, c]
        found += (at >= end).astype(jnp.int32)
    return found


def thirds(value):
    first = value.astype(BF16)
    value = value - first.astype(F32)
    second = value.astype(BF16)
    return [first.astype(F32), second.astype(F32), value - second.astype(F32)]


def over_entries(rows, chosen):
    return lax.dot_general(
        rows.astype(BF16), chosen, (((1,), (1,)), ((), ())), preferred_element_type=F32
    )


def plan_terms(group, source, coef, ints, floats):
    w, live = 128, group.shape[1]
    groups = lax.broadcasted_iota(jnp.int32, (w, live), 0)
    member = group == groups
    ones = jnp.where(member, 1.0, 0.0)
    earlier = lax.broadcasted_iota(jnp.int32, (live, live), 0) < lax.broadcasted_iota(
        jnp.int32, (live, live), 1
    )
    earlier = jnp.where(earlier, 1.0, 0.0).astype(BF16)
    before = product(ones.astype(BF16), earlier)
    size = jnp.sum(ones, axis=1, keepdims=True)
    rank = jnp.sum(ones * before, axis=0, keepdims=True)
    size_here = jnp.sum(ones * size, axis=0, keepdims=True)
    spilled = jnp.where(size_here > 2.0, jnp.where(rank > 0.0, 1.0, 0.0), 0.0)
    parts = thirds(coef)
    sources = source.astype(F32)
    zero = jnp.zeros_like(coef)
    rows = jnp.concatenate([sources, *parts, ones[0:1] * 0.0 + 1.0, zero, zero, zero], axis=0)
    first = over_entries(rows, jnp.where(before == 0.0, ones, 0.0).astype(BF16))
    second = over_entries(rows, jnp.where(before == 1.0, ones, 0.0).astype(BF16))
    large = over_entries(rows, ones.astype(BF16))[4:5] > 2.0
    at = lax.broadcasted_iota(jnp.int32, (1, w), 1)
    ints[0:1, 0:w] = first[0:1].astype(jnp.int32)
    ints[1:2, 0:w] = jnp.where(large, w + at, second[0:1].astype(jnp.int32))
    floats[0:1, 0:w] = first[1:2] + first[2:3] + first[3:4]
    floats[1:2, 0:w] = jnp.where(large, 1.0, second[1:2] + second[2:3] + second[3:4])

    place = product(jnp.concatenate([spilled] * 8, axis=0).astype(BF16), earlier)[0:1]
    place = jnp.where(spilled > 0.0, place, -1.0)
    column = lax.broadcasted_iota(jnp.int32, (live, live), 0).astype(F32)
    chosen = jnp.where(place == column, 1.0, 0.0).astype(BF16)
    again = jnp.where(rank > 1.0, 1.0, 0.0)
    rows = jnp.concatenate(
        [sources, *parts, (group + w).astype(F32), again, zero, zero], axis=0
    )
    listed = over_entries(rows, chosen)
    ints[2:3] = listed[0:1].astype(jnp.int32)
    count = jnp.sum(spilled)
    past = lax.broadcasted_iota(jnp.int32, (1, live), 1).astype(F32) >= count
    ints[3:4] = jnp.where(past, 2 * w, listed[4:5].astype(jnp.int32))
    ints[4:5] = jnp.full((1, live), count).astype(jnp.int32)
    floats[2:3] = listed[1:2] + listed[2:3] + listed[3:4]
    floats[3:4] = listed[5:6]


def spill(ints, floats, blocks):
    def add(q, unused):
        to = ints[3, q]
        held = jnp.where(floats[3, q] > 0.0, blocks[to], 0.0)
        blocks[to] = held + floats[2, q] * blocks[ints[2, q]]
        return unused

    def four(q, unused):
        for i in range(4):
            add(4 * q + i, unused)
        return unused

    lax.fori_loop(0, lax.div(ints[4, 0] + 3, 4), four, 0)


def two_terms(ints, floats, blocks, g):
    return floats[0, g] * blocks[ints[0, g]] + floats[1, g] * blocks[ints[1, g]]


def prepare_kernel(n, *refs):
    psi, given, refs = refs[0], refs[1:13], refs[13:]
    lefts, rights, up_ints, up_floats, mv_ints, mv_floats, own = refs[:7]
    held = refs[7:19]
    arrived, own_arrived = refs[19:]
    own_copy = pltpu.make_async_copy(psi.at[0, 0], own, own_arrived)
    own_copy.start()
    copies = [
        pltpu.make_async_copy(source, target, arrived.at[index])
        for index, (source, target) in enumerate(zip(given, held))
    ]
    for copy in copies:
        copy.start()
    up_counts, up_block, up_top, up_bot, up_coef = held[:5]
    mv_counts, mv_src, mv_dst, mv_coef, energies = held[5:10]
    left, right = held[10:]
    channels, w = left.shape[1], left.shape[2]
    live = up_block.shape[2]
    me = lax.axis_index("tile")
    for copy in copies[:10]:
        copy.wait()
    channel = channel_row(up_counts, live, channels)
    plan_terms(
        channel * n + (up_top[0] ^ me), up_block[0] * n + (up_bot[0] ^ me), up_coef[0], up_ints, up_floats
    )
    channel = channel_row(mv_counts, live, channels)
    plan_terms(
        channel * n + (mv_dst[0] ^ me), channel * n + (mv_src[0] ^ me), mv_coef[0], mv_ints, mv_floats
    )
    at = lax.broadcasted_iota(jnp.int32, (1, live), 1)
    by_slot = jnp.zeros((1, live), F32)
    for k in range(n):
        by_slot += jnp.where(at == k, energies[0, k ^ me], 0.0)
    mv_floats[4:5] = by_slot
    copies[10].wait()

    def halve_left(c, unused):
        lefts[pl.ds(pl.multiple_of(c * w, w), w)] = side_by_side(left[0, c])
        return unused

    lax.fori_loop(0, channels, halve_left, 0, unroll=2)
    copies[11].wait()

    def halve_right(c, unused):
        head, tail = heads_tails(right[0, c])
        rights[c, 0:w] = head
        rights[c, w : 2 * w] = tail
        return unused

    lax.fori_loop(0, channels, halve_right, 0, unroll=2)
    own_copy.wait()


def prepare_call(n, psi, given):
    channels, w = given[-1].shape[1], given[-1].shape[2]
    live = given[1].shape[2]
    table = (8, live)
    return pl.pallas_call(
        functools.partial(prepare_kernel, n),
        out_shape=(
            jax.ShapeDtypeStruct((channels * w, 2 * w), BF16),
            jax.ShapeDtypeStruct((channels, 2 * w, w), BF16),
            jax.ShapeDtypeStruct(table, jnp.int32),
            jax.ShapeDtypeStruct(table, F32),
            jax.ShapeDtypeStruct(table, jnp.int32),
            jax.ShapeDtypeStruct(table, F32),
            jax.ShapeDtypeStruct((w, w), F32),
        ),
        in_specs=[HBM] * (len(given) + 1),
        out_specs=(VMEM,) * 7,
        scratch_shapes=[
            *(
                pltpu.SMEM(x.shape, x.dtype) if x.shape[-1] in (channels, n) else pltpu.VMEM(x.shape, x.dtype)
                for x in given
            ),
            pltpu.SemaphoreType.DMA((len(given),)),
            pltpu.SemaphoreType.DMA,
        ],
        compiler_params=pltpu.CompilerParams(vmem_limit_bytes=12 << 20),
        cost_estimate=pl.CostEstimate(flops=10**9, bytes_accessed=6 << 20, transcendentals=0),
        name="prepare",
    )(*(pltpu.with_memory_space_constraint(x, pltpu.HBM) for x in (psi, *given)))


def fetch_tables(sources, targets, arrived):
    copies = [
        pltpu.make_async_copy(source, target, arrived.at[index])
        for index, (source, target) in enumerate(zip(sources, targets))
    ]
    for copy in copies:
        copy.start()
    return copies


def renew_kernel(n, *refs):
    tiles = [refs[ORDER.index(k)] for k in range(n)]
    lefts, int_table, float_table, out, bottoms, tops, entries, renewed, ints, floats, arrived, left = refs[n:]
    channels, w = out.shape[0], out.shape[1]
    copies = fetch_tables((int_table, float_table), (ints, floats), arrived)
    for k in range(n):
        at = slice(k * w, (k + 1) * w)
        value = tiles[k][...]
        head, tail = heads_tails(value)
        bottoms[0:w, at] = head
        bottoms[w : 2 * w, at] = head
        bottoms[2 * w : 3 * w, at] = tail
        bottoms[3 * w : 4 * w, at] = tail
        head, tail = heads_tails(value.T)
        tops[0:w, at] = head
        tops[w : 2 * w, at] = tail
    group = channels // 2

    def multiply(g, unused):
        own = lefts[pl.ds(pl.multiple_of(g * (group * w), group * w), group * w)]
        found = product(jnp.concatenate([own, own], axis=1), bottoms[...])
        for h in range(group):
            for k in range(n):
                entries[(g * group + h) * n + k] = found[h * w : (h + 1) * w, k * w : (k + 1) * w]
        return unused

    lax.fori_loop(0, 2, multiply, 0, unroll=2)
    for copy in copies:
        copy.wait()
    spill(ints, floats, entries)

    def finish(g, unused):
        heads, tails = [], []
        for b in (2 * g, 2 * g + 1):
            pairs = [heads_tails(two_terms(ints, floats, entries, b * n + k)) for k in range(n)]
            heads.append(jnp.concatenate([pair[0] for pair in pairs], axis=0))
            tails.append(jnp.concatenate([pair[1] for pair in pairs], axis=0))
        small = product(tops[w:], jnp.concatenate(heads, axis=1))
        for i in range(2):
            b = 2 * g + i
            found = product(tops[0:w], jnp.concatenate([heads[i], tails[i]], axis=1))
            renewed[b] = found[:, :w] + (found[:, w:] + small[:, i * w : (i + 1) * w])
            pltpu.make_async_copy(renewed.at[b], out.at[b], left.at[b]).start()
        return unused

    lax.fori_loop(0, channels // 2, finish, 0, unroll=4)
    for b in range(channels):
        pltpu.make_async_copy(renewed.at[b], out.at[b], left.at[b]).wait()


def renew_call(tiles, lefts, int_table, float_table, channels):
    n, w = len(tiles), tiles[0].shape[0]
    return pl.pallas_call(
        functools.partial(renew_kernel, n),
        out_shape=jax.ShapeDtypeStruct((channels, w, w), F32),
        in_specs=[VMEM] * (n + 1) + [ANY] * 2,
        out_specs=HBM,
        scratch_shapes=[
            pltpu.VMEM((4 * w, n * w), BF16),
            pltpu.VMEM((2 * w, n * w), BF16),
            pltpu.VMEM((2 * w + 1, w, w), F32),
            pltpu.VMEM((channels, w, w), F32),
            pltpu.SMEM(int_table.shape, jnp.int32),
            pltpu.SMEM(float_table.shape, F32),
            pltpu.SemaphoreType.DMA((2,)),
            pltpu.SemaphoreType.DMA((channels,)),
        ],
        compiler_params=pltpu.CompilerParams(vmem_limit_bytes=28 << 20),
        cost_estimate=pl.CostEstimate(flops=10**10, bytes_accessed=3 << 20, transcendentals=0),
        name="renew",
    )(*(tiles[k] for k in ORDER), lefts, int_table, float_table)


def source_kernel(n, *refs):
    tiles = refs[:n]
    rights, int_table, float_table, entries, stats, sources, ints, floats, arrived = refs[n:]
    channels, w = rights.shape[0], rights.shape[2]
    copies = fetch_tables((int_table, float_table), (ints, floats), arrived)
    for k in range(n):
        at = slice(k * w, (k + 1) * w)
        head, tail = heads_tails(tiles[k][...])
        sources[at, 0:w] = head
        sources[at, w : 2 * w] = tail
        sources[at, 2 * w : 3 * w] = head
        sources[at, 3 * w : 4 * w] = tail
    group = channels // 2

    def multiply(g, unused):
        columns = []
        for h in range(group):
            value = rights[g * group + h]
            columns.append(jnp.concatenate([value[:w], value[:w], value[w:], value[w:]], axis=0))
        found = product(sources[...], jnp.concatenate(columns, axis=1))
        for h in range(group):
            for k in range(n):
                entries[(g * group + h) * n + k] = found[k * w : (k + 1) * w, h * w : (h + 1) * w]
        return unused

    lax.fori_loop(0, 2, multiply, 0, unroll=2)
    for copy in copies:
        copy.wait()
    spill(ints, floats, entries)
    weight = jnp.zeros((8, w), F32)
    energy = jnp.zeros((8, w), F32)
    for k in range(n):
        value = tiles[k][...]
        squares = jnp.sum((value * value).reshape(w // 8, 8, w), axis=0)
        weight += squares
        energy += floats[4, k] * squares
    stats[0:8] = weight
    stats[8:16] = energy
    stats[16:24] = jnp.full((8, w), floats[4, 0], F32)


def source_call(tiles, rights, int_table, float_table):
    n, w = len(tiles), rights.shape[2]
    return pl.pallas_call(
        functools.partial(source_kernel, n),
        out_shape=(
            pltpu.VMEM((2 * w + 1, w, w), F32),
            jax.ShapeDtypeStruct((24, w), F32),
        ),
        in_specs=[VMEM] * (n + 1) + [ANY] * 2,
        out_specs=(VMEM, VMEM),
        scratch_shapes=[
            pltpu.VMEM((n * w, 4 * w), BF16),
            pltpu.SMEM(int_table.shape, jnp.int32),
            pltpu.SMEM(float_table.shape, F32),
            pltpu.SemaphoreType.DMA((2,)),
        ],
        compiler_params=pltpu.CompilerParams(vmem_limit_bytes=12 << 20),
        cost_estimate=pl.CostEstimate(flops=10**10, bytes_accessed=10 << 20, transcendentals=0),
        name="sources",
    )(*tiles, rights, int_table, float_table)


def apply_kernel(n, *refs):
    tiles = refs[:n]
    own, received, entries, int_table, float_table = refs[n : n + 5]
    outs = refs[n + 5 : 2 * n + 5]
    lefts, ints, floats, arrived = refs[2 * n + 5 :]
    channels, w = own.shape[0], own.shape[1]
    copies = fetch_tables((int_table, float_table), (ints, floats), arrived)
    leading = lax.axis_index("seg") == 0

    def halve(env):
        for c in range(channels):
            head, tail = heads_tails(env[c])
            lefts[0:w, c * w : (c + 1) * w] = head
            lefts[w : 2 * w, c * w : (c + 1) * w] = tail

    @pl.when(leading)
    def _():
        halve(own)

    @pl.when(jnp.logical_not(leading))
    def _():
        halve(received)

    for copy in copies:
        copy.wait()
    inner = jnp.zeros((8, w), F32)
    for k in range(0, n, 2):
        heads, tails = [], []
        for t in (k, k + 1):
            pairs = [
                heads_tails(two_terms(ints, floats, entries, c * n + t)) for c in range(channels)
            ]
            heads.append(jnp.concatenate([pair[0] for pair in pairs], axis=0))
            tails.append(jnp.concatenate([pair[1] for pair in pairs], axis=0))
        small = product(lefts[w:], jnp.concatenate(heads, axis=1))
        for i in range(2):
            found = product(lefts[0:w], jnp.concatenate([heads[i], tails[i]], axis=1))
            value = found[:, :w] + (found[:, w:] + small[:, i * w : (i + 1) * w])
            outs[k + i][0:w] = value
            inner += jnp.sum((value * tiles[k + i][...]).reshape(w // 8, 8, w), axis=0)
    for k in range(n):
        outs[k][w : w + 8] = inner


def apply_call(tiles, own, received, entries, int_table, float_table):
    n, w = len(tiles), own.shape[1]
    return pl.pallas_call(
        functools.partial(apply_kernel, n),
        out_shape=tuple(jax.ShapeDtypeStruct((w + 8, w), F32) for _ in range(n)),
        in_specs=[VMEM] * (n + 3) + [ANY] * 2,
        out_specs=(VMEM,) * n,
        scratch_shapes=[
            pltpu.VMEM((2 * w, own.shape[0] * w), BF16),
            pltpu.SMEM(int_table.shape, jnp.int32),
            pltpu.SMEM(float_table.shape, F32),
            pltpu.SemaphoreType.DMA((2,)),
        ],
        compiler_params=pltpu.CompilerParams(vmem_limit_bytes=12 << 20),
        cost_estimate=pl.CostEstimate(flops=5 * 10**9, bytes_accessed=10 << 20, transcendentals=0),
        name="applied",
    )(
        *tiles,
        own,
        received,
        pltpu.with_memory_space_constraint(entries, pltpu.VMEM),
        int_table,
        float_table,
    )


def finish_kernel(*refs):
    parts = refs[:-4]
    own, stats, residual, quotient = refs[-4:]
    w = own.shape[0]
    total = parts[0][...]
    for part in parts[1:]:
        total = total + part[...]
    value = own[...]
    numerator = jnp.sum(total[w : w + 8]) + jnp.sum(stats[8:16])
    ratio = jnp.full((1, 128), numerator, F32) / jnp.full((1, 128), jnp.sum(stats[0:8]), F32)
    residual[...] = total[:w] + (stats[16:17] - ratio) * value
    quotient[...] = ratio


def finish_call(parts, own, stats):
    w = own.shape[0]
    return pl.pallas_call(
        finish_kernel,
        out_shape=(jax.ShapeDtypeStruct((w, w), F32), jax.ShapeDtypeStruct((1, 128), F32)),
        in_specs=[VMEM] * (len(parts) + 2),
        out_specs=(VMEM, VMEM),
        compiler_params=pltpu.CompilerParams(vmem_limit_bytes=2 << 20),
        name="finish",
    )(*parts, own, stats)


def shards(
    psi,
    left_env,
    right_env,
    site_energy,
    mv_counts,
    mv_src,
    mv_dst,
    mv_coef,
    up_counts,
    up_block,
    up_top,
    up_bot,
    up_coef,
):
    n = lax.axis_size("tile")
    def across(value, k):
        return lax.ppermute(value, "tile", [(i, i ^ k) for i in range(n)])

    own = psi[0, 0]
    tiles = {k: across(own, k) for k in (1, 2, 3, 4, 6)}
    tiles[5], tiles[7] = across(tiles[4], 1), across(tiles[6], 1)

    given = [up_counts, up_block, up_top, up_bot, up_coef, mv_counts, mv_src, mv_dst, mv_coef, site_energy]
    lefts, rights, up_ints, up_floats, mv_ints, mv_floats, own = prepare_call(
        n, psi, [*given, left_env, right_env]
    )
    tiles[0] = own
    tiles = [tiles[k] for k in range(n)]
    renewal = renew_call(tiles, lefts, up_ints, up_floats, left_env.shape[1])
    received = lax.ppermute(renewal, "seg", [(0, 1), (1, 0)])
    entries, stats = source_call(tiles, rights, mv_ints, mv_floats)
    partials = apply_call(tiles, left_env[0], received, entries, mv_ints, mv_floats)

    parts = [partials[0], across(partials[1], 1)]
    for k in (2, 4, 6):
        parts.append(across(partials[k] + across(partials[k + 1], 1), k))
    residual, quotient = finish_call(parts, own, stats)
    return (residual[None, None], renewal[None], quotient[0, :1])


def solution(mesh):
    per_run = P(("parts", "seg"), "tile", None)
    return jax.shard_map(
        shards if mesh.shape["tile"] == 8 else general_shards,
        mesh=mesh,
        in_specs=(
            P(("parts", "seg"), "tile", None, None),
            P(("parts", "seg"), "tile", None, None),
            P(("parts", "seg"), "tile", None, None),
            P(("parts", "seg"), None),
            per_run,
            per_run,
            per_run,
            per_run,
            per_run,
            per_run,
            per_run,
            per_run,
            per_run,
        ),
        out_specs=(
            P(("parts", "seg"), "tile", None, None),
            P(("parts", "seg"), "tile", None, None),
            P(("parts", "seg")),
        ),
        check_vma=False,
    )
```

```python
import functools

import jax
import jax.numpy as jnp
from jax import lax
from jax.experimental import pallas as pl
from jax.experimental.pallas import tpu as pltpu
from jax.sharding import PartitionSpec as P

MAXT = 24
ORDER = (0, 7, 6, 5, 4, 1, 2, 3)
F32 = jnp.float32
BF16 = jnp.bfloat16
VMEM = pl.BlockSpec(memory_space=pltpu.VMEM)
SMEM = pl.BlockSpec(memory_space=pltpu.SMEM)
ANY = pl.BlockSpec(memory_space=pl.ANY)
HBM = pl.BlockSpec(memory_space=pltpu.HBM)


def passed_along(value, axis, steps):
    count = lax.axis_size(axis)
    first, last = (max(0, -steps), min(count, count - steps))
    return lax.ppermute(value, axis, [(source, source + steps) for source in range(first, last)])


def slot_layout(counts, most):
    block_ends = jnp.cumsum(counts)
    block_starts = block_ends - counts
    slots = jnp.arange(most, dtype=jnp.int32)
    live_slot = slots[None, :] < counts[:, None]
    slot_pos = jnp.where(live_slot, block_starts[:, None] + slots[None, :], 0)
    return (slot_pos, live_slot)


def apply_terms(gathered, env_used, right_own, counts, sources, targets, coefs):
    psi_count = gathered.shape[0]
    tile_width = gathered.shape[1]
    channels = counts.shape[0]
    quarter = channels // 4
    slot_pos, live_slot = slot_layout(counts, MAXT)
    src_slots = sources[slot_pos]
    dst_slots = targets[slot_pos]
    coef_slots = jnp.where(live_slot, coefs[slot_pos], 0.0)

    def apply_one_turn(running, inputs):
        env_part, right_part, src_part, dst_part, coef_part = inputs
        inner = jnp.einsum(
            "csij,cjk->csik", gathered[src_part], right_part, precision=lax.Precision.HIGHEST
        )
        contrib = jnp.einsum("cij,csjk->csik", env_part, inner, precision=lax.Precision.HIGHEST)
        contrib = contrib * coef_part[:, :, None, None]
        added = jax.ops.segment_sum(
            contrib.reshape(-1, tile_width, tile_width),
            dst_part.reshape(-1),
            num_segments=psi_count,
        )
        return (running + added, None)

    inputs = (
        env_used.reshape(4, quarter, tile_width, tile_width),
        right_own.reshape(4, quarter, tile_width, tile_width),
        src_slots.reshape(4, quarter, MAXT),
        dst_slots.reshape(4, quarter, MAXT),
        coef_slots.reshape(4, quarter, MAXT),
    )
    start_sum = jnp.zeros((psi_count, tile_width, tile_width), jnp.float32)
    summed, unused = lax.scan(apply_one_turn, start_sum, inputs)
    return summed


def renew_env(gathered, own_env, counts, blocks, tops, bottoms, coefs):
    tile_width = gathered.shape[1]
    channels = counts.shape[0]
    quarter = channels // 4
    slot_pos, live_slot = slot_layout(counts, MAXT)
    block_slots = blocks[slot_pos]
    top_slots = tops[slot_pos]
    bottom_slots = bottoms[slot_pos]
    coef_slots = jnp.where(live_slot, coefs[slot_pos], 0.0)

    def renew_one_turn(inputs):
        block_part, top_part, bottom_part, coef_part = inputs
        inner = jnp.einsum(
            "csij,csjk->csik",
            own_env[block_part],
            gathered[bottom_part],
            precision=lax.Precision.HIGHEST,
        )
        contrib = jnp.einsum(
            "csji,csjk->csik", gathered[top_part], inner, precision=lax.Precision.HIGHEST
        )
        contrib = contrib * coef_part[:, :, None, None]
        return jnp.sum(contrib, axis=1)

    inputs = (
        block_slots.reshape(4, quarter, MAXT),
        top_slots.reshape(4, quarter, MAXT),
        bottom_slots.reshape(4, quarter, MAXT),
        coef_slots.reshape(4, quarter, MAXT),
    )
    stacked = lax.map(renew_one_turn, inputs)
    return stacked.reshape(channels, tile_width, tile_width)


def general_shards(
    psi,
    left_env,
    right_env,
    site_energy,
    mv_counts,
    mv_src,
    mv_dst,
    mv_coef,
    up_counts,
    up_block,
    up_top,
    up_bot,
    up_coef,
):
    own_psi = psi[0]
    own_env = left_env[0]
    gathered = lax.all_gather(own_psi, "tile", axis=0, tiled=True)
    renewal = renew_env(
        gathered,
        own_env,
        up_counts[0, 0],
        up_block[0, 0],
        up_top[0, 0],
        up_bot[0, 0],
        up_coef[0, 0],
    )
    received = passed_along(renewal, "seg", 1)
    leading = lax.axis_index("seg") == 0
    env_used = jnp.where(leading, own_env, received)
    partial_value = apply_terms(
        gathered, env_used, right_env[0], mv_counts[0, 0], mv_src[0, 0], mv_dst[0, 0], mv_coef[0, 0]
    )
    row_count = own_psi.shape[0]
    energies = site_energy[0]
    row_start = lax.axis_index("tile") * row_count
    summed_own = lax.psum_scatter(partial_value, "tile", scatter_dimension=0, tiled=True)
    own_energy = lax.dynamic_slice_in_dim(energies, row_start, row_count, 0)
    own_rows = summed_own + own_energy[:, None, None] * own_psi
    numerator = lax.psum(jnp.sum(own_psi * own_rows), "tile")
    denominator = jnp.sum(gathered * gathered)
    quotient = numerator / denominator
    residual = own_rows - quotient * own_psi
    return (residual[None], renewal[None], jnp.reshape(quotient, (1,)))


def heads_tails(value):
    head = value.astype(BF16)
    return head, (value - head.astype(F32)).astype(BF16)


def side_by_side(value):
    return jnp.concatenate(heads_tails(value), axis=1)


def product(left, right):
    return jnp.dot(left, right, preferred_element_type=F32)


def channel_row(counts, live, channels):
    at = lax.broadcasted_iota(jnp.int32, (1, live), 1)
    found = jnp.zeros((1, live), jnp.int32)
    end = 0
    for c in range(channels):
        end = end + counts[0, 0, c]
        found += (at >= end).astype(jnp.int32)
    return found


def thirds(value):
    first = value.astype(BF16)
    value = value - first.astype(F32)
    second = value.astype(BF16)
    return [first.astype(F32), second.astype(F32), value - second.astype(F32)]


def over_entries(rows, chosen):
    return lax.dot_general(
        rows.astype(BF16), chosen, (((1,), (1,)), ((), ())), preferred_element_type=F32
    )


def plan_terms(group, source, coef, ints, floats):
    w, live = 128, group.shape[1]
    groups = lax.broadcasted_iota(jnp.int32, (w, live), 0)
    member = group == groups
    ones = jnp.where(member, 1.0, 0.0)
    earlier = lax.broadcasted_iota(jnp.int32, (live, live), 0) < lax.broadcasted_iota(
        jnp.int32, (live, live), 1
    )
    earlier = jnp.where(earlier, 1.0, 0.0).astype(BF16)
    before = product(ones.astype(BF16), earlier)
    size = jnp.sum(ones, axis=1, keepdims=True)
    rank = jnp.sum(ones * before, axis=0, keepdims=True)
    size_here = jnp.sum(ones * size, axis=0, keepdims=True)
    spilled = jnp.where(size_here > 2.0, jnp.where(rank > 0.0, 1.0, 0.0), 0.0)
    parts = thirds(coef)
    sources = source.astype(F32)
    zero = jnp.zeros_like(coef)
    rows = jnp.concatenate([sources, *parts, ones[0:1] * 0.0 + 1.0, zero, zero, zero], axis=0)
    first = over_entries(rows, jnp.where(before == 0.0, ones, 0.0).astype(BF16))
    second = over_entries(rows, jnp.where(before == 1.0, ones, 0.0).astype(BF16))
    large = over_entries(rows, ones.astype(BF16))[4:5] > 2.0
    at = lax.broadcasted_iota(jnp.int32, (1, w), 1)
    ints[0:1, 0:w] = first[0:1].astype(jnp.int32)
    ints[1:2, 0:w] = jnp.where(large, w + at, second[0:1].astype(jnp.int32))
    floats[0:1, 0:w] = first[1:2] + first[2:3] + first[3:4]
    floats[1:2, 0:w] = jnp.where(large, 1.0, second[1:2] + second[2:3] + second[3:4])

    place = product(jnp.concatenate([spilled] * 8, axis=0).astype(BF16), earlier)[0:1]
    place = jnp.where(spilled > 0.0, place, -1.0)
    column = lax.broadcasted_iota(jnp.int32, (live, live), 0).astype(F32)
    chosen = jnp.where(place == column, 1.0, 0.0).astype(BF16)
    again = jnp.where(rank > 1.0, 1.0, 0.0)
    rows = jnp.concatenate(
        [sources, *parts, (group + w).astype(F32), again, zero, zero], axis=0
    )
    listed = over_entries(rows, chosen)
    ints[2:3] = listed[0:1].astype(jnp.int32)
    count = jnp.sum(spilled)
    past = lax.broadcasted_iota(jnp.int32, (1, live), 1).astype(F32) >= count
    ints[3:4] = jnp.where(past, 2 * w, listed[4:5].astype(jnp.int32))
    ints[4:5] = jnp.full((1, live), count).astype(jnp.int32)
    floats[2:3] = listed[1:2] + listed[2:3] + listed[3:4]
    floats[3:4] = listed[5:6]


def spill(ints, floats, blocks):
    def add(q, unused):
        to = ints[3, q]
        held = jnp.where(floats[3, q] > 0.0, blocks[to], 0.0)
        blocks[to] = held + floats[2, q] * blocks[ints[2, q]]
        return unused

    def four(q, unused):
        for i in range(4):
            add(4 * q + i, unused)
        return unused

    lax.fori_loop(0, lax.div(ints[4, 0] + 3, 4), four, 0)


def two_terms(ints, floats, blocks, g):
    return floats[0, g] * blocks[ints[0, g]] + floats[1, g] * blocks[ints[1, g]]


def stack_halves(tile, stacked, k):
    w = tile.shape[0]
    at = slice(k * w, (k + 1) * w)
    head, tail = heads_tails(tile[...])
    stacked[0:w, at] = head
    stacked[w : 2 * w, at] = head
    stacked[2 * w : 3 * w, at] = tail
    stacked[3 * w : 4 * w, at] = tail


def multiply_blocks(lefts, stacked, entries, n, first):
    w = lefts.shape[1] // 2
    count = stacked.shape[1] // w
    group = lefts.shape[0] // w // 2

    def multiply(g, unused):
        own = lefts[pl.ds(pl.multiple_of(g * (group * w), group * w), group * w)]
        found = product(jnp.concatenate([own, own], axis=1), stacked[...])
        for h in range(group):
            for k in range(count):
                entries[(g * group + h) * n + first + k] = found[
                    h * w : (h + 1) * w, k * w : (k + 1) * w
                ]
        return unused

    lax.fori_loop(0, 2, multiply, 0, unroll=2)


def prepare_kernel(n, *refs):
    psi, given, near, refs = refs[0], refs[1:13], refs[13 : 12 + n // 2], refs[12 + n // 2 :]
    lefts, rights, up_ints, up_floats, mv_ints, mv_floats, own, entries = refs[:8]
    held = refs[8:20]
    bottoms, arrived, own_arrived = refs[20:]
    own_copy = pltpu.make_async_copy(psi.at[0, 0], own, own_arrived)
    own_copy.start()
    copies = [
        pltpu.make_async_copy(source, target, arrived.at[index])
        for index, (source, target) in enumerate(zip(given, held))
    ]
    for copy in copies:
        copy.start()
    up_counts, up_block, up_top, up_bot, up_coef = held[:5]
    mv_counts, mv_src, mv_dst, mv_coef, energies = held[5:10]
    left, right = held[10:]
    channels, w = left.shape[1], left.shape[2]
    live = up_block.shape[2]
    me = lax.axis_index("tile")
    for copy in copies[:10]:
        copy.wait()
    channel = channel_row(up_counts, live, channels)
    plan_terms(
        channel * n + (up_top[0] ^ me), up_block[0] * n + (up_bot[0] ^ me), up_coef[0], up_ints, up_floats
    )
    channel = channel_row(mv_counts, live, channels)
    plan_terms(
        channel * n + (mv_dst[0] ^ me), channel * n + (mv_src[0] ^ me), mv_coef[0], mv_ints, mv_floats
    )
    at = lax.broadcasted_iota(jnp.int32, (1, live), 1)
    by_slot = jnp.zeros((1, live), F32)
    for k in range(n):
        by_slot += jnp.where(at == k, energies[0, k ^ me], 0.0)
    mv_floats[4:5] = by_slot
    copies[10].wait()

    def halve_left(c, unused):
        lefts[pl.ds(pl.multiple_of(c * w, w), w)] = side_by_side(left[0, c])
        return unused

    lax.fori_loop(0, channels, halve_left, 0, unroll=2)
    copies[11].wait()

    def halve_right(c, unused):
        head, tail = heads_tails(right[0, c])
        rights[c, 0:w] = head
        rights[c, w : 2 * w] = tail
        return unused

    lax.fori_loop(0, channels, halve_right, 0, unroll=2)
    own_copy.wait()
    for k, tile in enumerate((own, *near)):
        stack_halves(tile, bottoms, k)
    multiply_blocks(lefts, bottoms, entries, n, 0)


def prepare_call(n, psi, given, near):
    channels, w = given[-1].shape[1], given[-1].shape[2]
    live = given[1].shape[2]
    table = (8, live)
    return pl.pallas_call(
        functools.partial(prepare_kernel, n),
        out_shape=(
            jax.ShapeDtypeStruct((channels * w, 2 * w), BF16),
            jax.ShapeDtypeStruct((channels, 2 * w, w), BF16),
            jax.ShapeDtypeStruct(table, jnp.int32),
            jax.ShapeDtypeStruct(table, F32),
            jax.ShapeDtypeStruct(table, jnp.int32),
            jax.ShapeDtypeStruct(table, F32),
            jax.ShapeDtypeStruct((w, w), F32),
            pltpu.VMEM((2 * w + 1, w, w), F32),
        ),
        in_specs=[HBM] * (len(given) + 1) + [VMEM] * len(near),
        out_specs=(VMEM,) * 8,
        scratch_shapes=[
            *(
                pltpu.SMEM(x.shape, x.dtype) if x.shape[-1] in (channels, n) else pltpu.VMEM(x.shape, x.dtype)
                for x in given
            ),
            pltpu.VMEM((4 * w, n // 2 * w), BF16),
            pltpu.SemaphoreType.DMA((len(given),)),
            pltpu.SemaphoreType.DMA,
        ],
        compiler_params=pltpu.CompilerParams(vmem_limit_bytes=16 << 20),
        cost_estimate=pl.CostEstimate(flops=10**9, bytes_accessed=6 << 20, transcendentals=0),
        name="prepare",
    )(*(pltpu.with_memory_space_constraint(x, pltpu.HBM) for x in (psi, *given)), *near)


def fetch_tables(sources, targets, arrived):
    copies = [
        pltpu.make_async_copy(source, target, arrived.at[index])
        for index, (source, target) in enumerate(zip(sources, targets))
    ]
    for copy in copies:
        copy.start()
    return copies


def renew_kernel(n, *refs):
    tiles = [refs[ORDER.index(k)] for k in range(n)]
    lefts, int_table, float_table, _, renewed, entries, bottoms, tops, ints, floats, arrived = refs[n:]
    channels, w = renewed.shape[0], renewed.shape[1]
    copies = fetch_tables((int_table, float_table), (ints, floats), arrived)
    for k in range(n // 2):
        stack_halves(tiles[n // 2 + k], bottoms, k)
    multiply_blocks(lefts, bottoms, entries, n, n // 2)
    for k in range(n):
        at = slice(k * w, (k + 1) * w)
        head, tail = heads_tails(tiles[k][...].T)
        tops[0:w, at] = head
        tops[w : 2 * w, at] = tail
    for copy in copies:
        copy.wait()
    spill(ints, floats, entries)

    def finish(g, unused):
        heads, tails = [], []
        for b in (2 * g, 2 * g + 1):
            pairs = [heads_tails(two_terms(ints, floats, entries, b * n + k)) for k in range(n)]
            heads.append(jnp.concatenate([pair[0] for pair in pairs], axis=0))
            tails.append(jnp.concatenate([pair[1] for pair in pairs], axis=0))
        small = product(tops[w:], jnp.concatenate(heads, axis=1))
        for i in range(2):
            b = 2 * g + i
            found = product(tops[0:w], jnp.concatenate([heads[i], tails[i]], axis=1))
            renewed[b] = found[:, :w] + (found[:, w:] + small[:, i * w : (i + 1) * w])
        return unused

    lax.fori_loop(0, channels // 2, finish, 0, unroll=4)


def renew_call(tiles, lefts, int_table, float_table, entries, channels):
    n, w = len(tiles), tiles[0].shape[0]
    return pl.pallas_call(
        functools.partial(renew_kernel, n),
        out_shape=(pltpu.VMEM((channels, w, w), F32), pltpu.VMEM(entries.shape, F32)),
        in_specs=[VMEM] * (n + 1) + [ANY] * 2 + [VMEM],
        out_specs=(VMEM, VMEM),
        input_output_aliases={n + 3: 1},
        scratch_shapes=[
            pltpu.VMEM((4 * w, n // 2 * w), BF16),
            pltpu.VMEM((2 * w, n * w), BF16),
            pltpu.SMEM(int_table.shape, jnp.int32),
            pltpu.SMEM(float_table.shape, F32),
            pltpu.SemaphoreType.DMA((2,)),
        ],
        compiler_params=pltpu.CompilerParams(vmem_limit_bytes=12 << 20),
        cost_estimate=pl.CostEstimate(flops=10**10, bytes_accessed=3 << 20, transcendentals=0),
        name="renew",
    )(
        *(tiles[k] for k in ORDER),
        lefts,
        int_table,
        float_table,
        pltpu.with_memory_space_constraint(entries, pltpu.VMEM),
    )[0]


def source_kernel(n, *refs):
    tiles = [refs[ORDER.index(k)] for k in range(n)]
    rights, int_table, float_table, entries, stats, sources, ints, floats, arrived = refs[n:]
    channels, w = rights.shape[0], rights.shape[2]
    copies = fetch_tables((int_table, float_table), (ints, floats), arrived)
    for k in range(n):
        at = slice(k * w, (k + 1) * w)
        head, tail = heads_tails(tiles[k][...])
        sources[at, 0:w] = head
        sources[at, w : 2 * w] = tail
        sources[at, 2 * w : 3 * w] = head
        sources[at, 3 * w : 4 * w] = tail
    group = channels // 2

    def multiply(g, unused):
        columns = []
        for h in range(group):
            value = rights[g * group + h]
            columns.append(jnp.concatenate([value[:w], value[:w], value[w:], value[w:]], axis=0))
        found = product(sources[...], jnp.concatenate(columns, axis=1))
        for h in range(group):
            for k in range(n):
                entries[(g * group + h) * n + k] = found[k * w : (k + 1) * w, h * w : (h + 1) * w]
        return unused

    lax.fori_loop(0, 2, multiply, 0, unroll=2)
    for copy in copies:
        copy.wait()
    spill(ints, floats, entries)
    weight = jnp.zeros((8, w), F32)
    energy = jnp.zeros((8, w), F32)
    for k in range(n):
        value = tiles[k][...]
        squares = jnp.sum((value * value).reshape(w // 8, 8, w), axis=0)
        weight += squares
        energy += floats[4, k] * squares
    stats[0:8] = weight
    stats[8:16] = energy
    stats[16:24] = jnp.full((8, w), floats[4, 0], F32)


def source_call(tiles, rights, int_table, float_table):
    n, w = len(tiles), rights.shape[2]
    return pl.pallas_call(
        functools.partial(source_kernel, n),
        out_shape=(
            pltpu.VMEM((2 * w + 1, w, w), F32),
            jax.ShapeDtypeStruct((24, w), F32),
        ),
        in_specs=[VMEM] * (n + 1) + [ANY] * 2,
        out_specs=(VMEM, VMEM),
        scratch_shapes=[
            pltpu.VMEM((n * w, 4 * w), BF16),
            pltpu.SMEM(int_table.shape, jnp.int32),
            pltpu.SMEM(float_table.shape, F32),
            pltpu.SemaphoreType.DMA((2,)),
        ],
        compiler_params=pltpu.CompilerParams(vmem_limit_bytes=12 << 20),
        cost_estimate=pl.CostEstimate(flops=10**10, bytes_accessed=10 << 20, transcendentals=0),
        name="sources",
    )(*(tiles[k] for k in ORDER), rights, int_table, float_table)


def apply_kernel(n, *refs):
    tiles = [refs[ORDER.index(k)] for k in range(n)]
    own, received, entries, int_table, float_table = refs[n : n + 5]
    outs = refs[n + 5 : 2 * n + 5]
    lefts, ints, floats, arrived = refs[2 * n + 5 :]
    channels, w = own.shape[0], own.shape[1]
    copies = fetch_tables((int_table, float_table), (ints, floats), arrived)
    leading = lax.axis_index("seg") == 0

    def halve(env):
        for c in range(channels):
            head, tail = heads_tails(env[c])
            lefts[0:w, c * w : (c + 1) * w] = head
            lefts[w : 2 * w, c * w : (c + 1) * w] = tail

    @pl.when(leading)
    def _():
        halve(own)

    @pl.when(jnp.logical_not(leading))
    def _():
        halve(received)

    for copy in copies:
        copy.wait()
    inner = jnp.zeros((8, w), F32)
    for k in range(0, n, 2):
        heads, tails = [], []
        for t in (k, k + 1):
            pairs = [
                heads_tails(two_terms(ints, floats, entries, c * n + t)) for c in range(channels)
            ]
            heads.append(jnp.concatenate([pair[0] for pair in pairs], axis=0))
            tails.append(jnp.concatenate([pair[1] for pair in pairs], axis=0))
        small = product(lefts[w:], jnp.concatenate(heads, axis=1))
        for i in range(2):
            found = product(lefts[0:w], jnp.concatenate([heads[i], tails[i]], axis=1))
            value = found[:, :w] + (found[:, w:] + small[:, i * w : (i + 1) * w])
            outs[k + i][0:w] = value
            inner += jnp.sum((value * tiles[k + i][...]).reshape(w // 8, 8, w), axis=0)
    for k in range(n):
        outs[k][w : w + 8] = inner


def apply_call(tiles, own, received, entries, int_table, float_table):
    n, w = len(tiles), own.shape[1]
    return pl.pallas_call(
        functools.partial(apply_kernel, n),
        out_shape=tuple(jax.ShapeDtypeStruct((w + 8, w), F32) for _ in range(n)),
        in_specs=[VMEM] * (n + 3) + [ANY] * 2,
        out_specs=(VMEM,) * n,
        scratch_shapes=[
            pltpu.VMEM((2 * w, own.shape[0] * w), BF16),
            pltpu.SMEM(int_table.shape, jnp.int32),
            pltpu.SMEM(float_table.shape, F32),
            pltpu.SemaphoreType.DMA((2,)),
        ],
        compiler_params=pltpu.CompilerParams(vmem_limit_bytes=12 << 20),
        cost_estimate=pl.CostEstimate(flops=5 * 10**9, bytes_accessed=10 << 20, transcendentals=0),
        name="applied",
    )(
        *(tiles[k] for k in ORDER),
        own,
        received,
        pltpu.with_memory_space_constraint(entries, pltpu.VMEM),
        int_table,
        float_table,
    )


def finish_kernel(*refs):
    parts = refs[:-4]
    own, stats, residual, quotient = refs[-4:]
    w = own.shape[0]
    total = parts[0][...]
    for part in parts[1:]:
        total = total + part[...]
    value = own[...]
    numerator = jnp.sum(total[w : w + 8]) + jnp.sum(stats[8:16])
    ratio = jnp.full((1, 128), numerator, F32) / jnp.full((1, 128), jnp.sum(stats[0:8]), F32)
    residual[...] = total[:w] + (stats[16:17] - ratio) * value
    quotient[...] = ratio


def finish_call(parts, own, stats):
    w = own.shape[0]
    return pl.pallas_call(
        finish_kernel,
        out_shape=(jax.ShapeDtypeStruct((w, w), F32), jax.ShapeDtypeStruct((1, 128), F32)),
        in_specs=[VMEM] * (len(parts) + 2),
        out_specs=(VMEM, VMEM),
        compiler_params=pltpu.CompilerParams(vmem_limit_bytes=2 << 20),
        name="finish",
    )(*parts, own, stats)


def shards(
    psi,
    left_env,
    right_env,
    site_energy,
    mv_counts,
    mv_src,
    mv_dst,
    mv_coef,
    up_counts,
    up_block,
    up_top,
    up_bot,
    up_coef,
):
    n = lax.axis_size("tile")
    def across(value, k):
        return lax.ppermute(value, "tile", [(i, i ^ k) for i in range(n)])

    own = psi[0, 0]
    half = n // 2
    tiles = {k: across(own, k) for k in range(1, half + 1)}
    for k in range(1, half):
        tiles[half + k] = across(tiles[half], k)

    given = [up_counts, up_block, up_top, up_bot, up_coef, mv_counts, mv_src, mv_dst, mv_coef, site_energy]
    lefts, rights, up_ints, up_floats, mv_ints, mv_floats, own, products = prepare_call(
        n, psi, [*given, left_env, right_env], [tiles[k] for k in range(1, half)]
    )
    tiles[0] = own
    tiles = [tiles[k] for k in range(n)]
    renewal = renew_call(tiles, lefts, up_ints, up_floats, products, left_env.shape[1])
    received = lax.ppermute(renewal, "seg", [(0, 1), (1, 0)])
    entries, stats = source_call(tiles, rights, mv_ints, mv_floats)
    partials = apply_call(tiles, left_env[0], received, entries, mv_ints, mv_floats)

    far = partials[half]
    for k in range(half - 1, 0, -1):
        far = far + across(partials[half + k], k)
    far = across(far, half)
    parts = [partials[0], *(across(partials[k], k) for k in range(half - 1, 0, -1)), far]
    residual, quotient = finish_call(parts, own, stats)
    return (residual[None, None], renewal[None], quotient[0, :1])


def solution(mesh):
    per_run = P(("parts", "seg"), "tile", None)
    return jax.shard_map(
        shards if mesh.shape["tile"] == 8 else general_shards,
        mesh=mesh,
        in_specs=(
            P(("parts", "seg"), "tile", None, None),
            P(("parts", "seg"), "tile", None, None),
            P(("parts", "seg"), "tile", None, None),
            P(("parts", "seg"), None),
            per_run,
            per_run,
            per_run,
            per_run,
            per_run,
            per_run,
            per_run,
            per_run,
            per_run,
        ),
        out_specs=(
            P(("parts", "seg"), "tile", None, None),
            P(("parts", "seg"), "tile", None, None),
            P(("parts", "seg")),
        ),
        check_vma=False,
    )
```

```python
import functools

import jax
import jax.numpy as jnp
from jax import lax
from jax.experimental import pallas as pl
from jax.experimental.pallas import tpu as pltpu
from jax.sharding import PartitionSpec as P

MAXT = 24
ORDER = (0, 7, 6, 5, 4, 1, 2, 3)
F32 = jnp.float32
BF16 = jnp.bfloat16
VMEM = pl.BlockSpec(memory_space=pltpu.VMEM)
SMEM = pl.BlockSpec(memory_space=pltpu.SMEM)
ANY = pl.BlockSpec(memory_space=pl.ANY)
HBM = pl.BlockSpec(memory_space=pltpu.HBM)


def passed_along(value, axis, steps):
    count = lax.axis_size(axis)
    first, last = (max(0, -steps), min(count, count - steps))
    return lax.ppermute(value, axis, [(source, source + steps) for source in range(first, last)])


def slot_layout(counts, most):
    block_ends = jnp.cumsum(counts)
    block_starts = block_ends - counts
    slots = jnp.arange(most, dtype=jnp.int32)
    live_slot = slots[None, :] < counts[:, None]
    slot_pos = jnp.where(live_slot, block_starts[:, None] + slots[None, :], 0)
    return (slot_pos, live_slot)


def apply_terms(gathered, env_used, right_own, counts, sources, targets, coefs):
    psi_count = gathered.shape[0]
    tile_width = gathered.shape[1]
    channels = counts.shape[0]
    quarter = channels // 4
    slot_pos, live_slot = slot_layout(counts, MAXT)
    src_slots = sources[slot_pos]
    dst_slots = targets[slot_pos]
    coef_slots = jnp.where(live_slot, coefs[slot_pos], 0.0)

    def apply_one_turn(running, inputs):
        env_part, right_part, src_part, dst_part, coef_part = inputs
        inner = jnp.einsum(
            "csij,cjk->csik", gathered[src_part], right_part, precision=lax.Precision.HIGHEST
        )
        contrib = jnp.einsum("cij,csjk->csik", env_part, inner, precision=lax.Precision.HIGHEST)
        contrib = contrib * coef_part[:, :, None, None]
        added = jax.ops.segment_sum(
            contrib.reshape(-1, tile_width, tile_width),
            dst_part.reshape(-1),
            num_segments=psi_count,
        )
        return (running + added, None)

    inputs = (
        env_used.reshape(4, quarter, tile_width, tile_width),
        right_own.reshape(4, quarter, tile_width, tile_width),
        src_slots.reshape(4, quarter, MAXT),
        dst_slots.reshape(4, quarter, MAXT),
        coef_slots.reshape(4, quarter, MAXT),
    )
    start_sum = jnp.zeros((psi_count, tile_width, tile_width), jnp.float32)
    summed, unused = lax.scan(apply_one_turn, start_sum, inputs)
    return summed


def renew_env(gathered, own_env, counts, blocks, tops, bottoms, coefs):
    tile_width = gathered.shape[1]
    channels = counts.shape[0]
    quarter = channels // 4
    slot_pos, live_slot = slot_layout(counts, MAXT)
    block_slots = blocks[slot_pos]
    top_slots = tops[slot_pos]
    bottom_slots = bottoms[slot_pos]
    coef_slots = jnp.where(live_slot, coefs[slot_pos], 0.0)

    def renew_one_turn(inputs):
        block_part, top_part, bottom_part, coef_part = inputs
        inner = jnp.einsum(
            "csij,csjk->csik",
            own_env[block_part],
            gathered[bottom_part],
            precision=lax.Precision.HIGHEST,
        )
        contrib = jnp.einsum(
            "csji,csjk->csik", gathered[top_part], inner, precision=lax.Precision.HIGHEST
        )
        contrib = contrib * coef_part[:, :, None, None]
        return jnp.sum(contrib, axis=1)

    inputs = (
        block_slots.reshape(4, quarter, MAXT),
        top_slots.reshape(4, quarter, MAXT),
        bottom_slots.reshape(4, quarter, MAXT),
        coef_slots.reshape(4, quarter, MAXT),
    )
    stacked = lax.map(renew_one_turn, inputs)
    return stacked.reshape(channels, tile_width, tile_width)


def general_shards(
    psi,
    left_env,
    right_env,
    site_energy,
    mv_counts,
    mv_src,
    mv_dst,
    mv_coef,
    up_counts,
    up_block,
    up_top,
    up_bot,
    up_coef,
):
    own_psi = psi[0]
    own_env = left_env[0]
    gathered = lax.all_gather(own_psi, "tile", axis=0, tiled=True)
    renewal = renew_env(
        gathered,
        own_env,
        up_counts[0, 0],
        up_block[0, 0],
        up_top[0, 0],
        up_bot[0, 0],
        up_coef[0, 0],
    )
    received = passed_along(renewal, "seg", 1)
    leading = lax.axis_index("seg") == 0
    env_used = jnp.where(leading, own_env, received)
    partial_value = apply_terms(
        gathered, env_used, right_env[0], mv_counts[0, 0], mv_src[0, 0], mv_dst[0, 0], mv_coef[0, 0]
    )
    row_count = own_psi.shape[0]
    energies = site_energy[0]
    row_start = lax.axis_index("tile") * row_count
    summed_own = lax.psum_scatter(partial_value, "tile", scatter_dimension=0, tiled=True)
    own_energy = lax.dynamic_slice_in_dim(energies, row_start, row_count, 0)
    own_rows = summed_own + own_energy[:, None, None] * own_psi
    numerator = lax.psum(jnp.sum(own_psi * own_rows), "tile")
    denominator = jnp.sum(gathered * gathered)
    quotient = numerator / denominator
    residual = own_rows - quotient * own_psi
    return (residual[None], renewal[None], jnp.reshape(quotient, (1,)))


def heads_tails(value):
    head = value.astype(BF16)
    return head, (value - head.astype(F32)).astype(BF16)


def side_by_side(value):
    return jnp.concatenate(heads_tails(value), axis=1)


def product(left, right):
    return jnp.dot(left, right, preferred_element_type=F32)


def channel_row(counts, live, channels):
    at = lax.broadcasted_iota(jnp.int32, (1, live), 1)
    found = jnp.zeros((1, live), jnp.int32)
    end = 0
    for c in range(channels):
        end = end + counts[0, 0, c]
        found += (at >= end).astype(jnp.int32)
    return found


def thirds(value):
    first = value.astype(BF16)
    value = value - first.astype(F32)
    second = value.astype(BF16)
    return [first.astype(F32), second.astype(F32), value - second.astype(F32)]


def over_entries(rows, chosen):
    return lax.dot_general(
        rows.astype(BF16), chosen, (((1,), (1,)), ((), ())), preferred_element_type=F32
    )


def plan_terms(group, source, coef, ints, floats):
    w, live = 128, group.shape[1]
    groups = lax.broadcasted_iota(jnp.int32, (w, live), 0)
    member = group == groups
    ones = jnp.where(member, 1.0, 0.0)
    earlier = lax.broadcasted_iota(jnp.int32, (live, live), 0) < lax.broadcasted_iota(
        jnp.int32, (live, live), 1
    )
    earlier = jnp.where(earlier, 1.0, 0.0).astype(BF16)
    before = product(ones.astype(BF16), earlier)
    size = jnp.sum(ones, axis=1, keepdims=True)
    rank = jnp.sum(ones * before, axis=0, keepdims=True)
    size_here = jnp.sum(ones * size, axis=0, keepdims=True)
    spilled = jnp.where(size_here > 2.0, jnp.where(rank > 0.0, 1.0, 0.0), 0.0)
    parts = thirds(coef)
    sources = source.astype(F32)
    zero = jnp.zeros_like(coef)
    rows = jnp.concatenate([sources, *parts, ones[0:1] * 0.0 + 1.0, zero, zero, zero], axis=0)
    first = over_entries(rows, jnp.where(before == 0.0, ones, 0.0).astype(BF16))
    second = over_entries(rows, jnp.where(before == 1.0, ones, 0.0).astype(BF16))
    large = over_entries(rows, ones.astype(BF16))[4:5] > 2.0
    at = lax.broadcasted_iota(jnp.int32, (1, w), 1)
    ints[0:1, 0:w] = first[0:1].astype(jnp.int32)
    ints[1:2, 0:w] = jnp.where(large, w + at, second[0:1].astype(jnp.int32))
    floats[0:1, 0:w] = first[1:2] + first[2:3] + first[3:4]
    floats[1:2, 0:w] = jnp.where(large, 1.0, second[1:2] + second[2:3] + second[3:4])

    twos = jnp.where(size > 2.0, jnp.floor(size * 0.5), 0.0)
    column = lax.broadcasted_iota(jnp.int32, (w, w), 0)
    lower = jnp.where(lax.broadcasted_iota(jnp.int32, (w, w), 1) < column, 1.0, 0.0).astype(BF16)
    start = product(lower, jnp.broadcast_to(twos, (w, w)).astype(BF16))[:, 0:1]
    count = jnp.sum(twos)
    two = jnp.floor((rank - 1.0) * 0.5)
    second = rank - 1.0 - 2.0 * two
    place = jnp.sum(ones * start, axis=0, keepdims=True) + two
    place = jnp.where(spilled > 0.0, place, -1.0)
    column = lax.broadcasted_iota(jnp.int32, (live, live), 0).astype(F32)
    chosen = jnp.where(place == column, 1.0, 0.0)
    again = jnp.where(two > 0.0, 1.0, 0.0)
    rows = jnp.concatenate(
        [sources, *parts, (group + w).astype(F32), again, zero, zero], axis=0
    )
    past = lax.broadcasted_iota(jnp.int32, (1, live), 1).astype(F32) >= count
    for i in range(2):
        listed = over_entries(rows, (chosen * jnp.where(second == i, 1.0, 0.0)).astype(BF16))
        ints[2 + i : 3 + i] = listed[0:1].astype(jnp.int32)
        floats[2 + i : 3 + i] = listed[1:2] + listed[2:3] + listed[3:4]
        if i == 0:
            ints[4:5] = jnp.where(past, 2 * w, listed[4:5].astype(jnp.int32))
            floats[5:6] = listed[5:6]
    ints[5:6] = jnp.full((1, live), count).astype(jnp.int32)


def spill(ints, floats, blocks):
    def add(q):
        to = ints[4, q]
        held = jnp.where(floats[5, q] > 0.0, blocks[to], 0.0)
        pair = floats[2, q] * blocks[ints[2, q]] + floats[3, q] * blocks[ints[3, q]]
        blocks[to] = held + pair

    def four(q, unused):
        for i in range(4):
            add(4 * q + i)
        return unused

    lax.fori_loop(0, lax.div(ints[5, 0] + 3, 4), four, 0)


def two_terms(ints, floats, blocks, g):
    return floats[0, g] * blocks[ints[0, g]] + floats[1, g] * blocks[ints[1, g]]


def stack_halves(tile, stacked, k):
    w = tile.shape[0]
    at = slice(k * w, (k + 1) * w)
    head, tail = heads_tails(tile[...])
    stacked[0:w, at] = head
    stacked[w : 2 * w, at] = head
    stacked[2 * w : 3 * w, at] = tail
    stacked[3 * w : 4 * w, at] = tail


def multiply_blocks(lefts, stacked, entries, n, first, parts=2):
    w = lefts.shape[1] // 2
    count = stacked.shape[1] // w
    group = lefts.shape[0] // w // parts

    def multiply(g, unused):
        own = lefts[pl.ds(pl.multiple_of(g * (group * w), group * w), group * w)]
        found = product(jnp.concatenate([own, own], axis=1), stacked[...])
        for h in range(group):
            for k in range(count):
                entries[(g * group + h) * n + first + k] = found[
                    h * w : (h + 1) * w, k * w : (k + 1) * w
                ]
        return unused

    lax.fori_loop(0, parts, multiply, 0, unroll=parts)


def prepare_kernel(n, *refs):
    psi, given, refs = refs[0], refs[1:13], refs[13:]
    near, refs = refs[: n // 2 - 1], refs[n // 2 - 1 :]
    lefts, rights, up_ints, up_floats, mv_ints, mv_floats, own, up_entries = refs[:8]
    held, refs = refs[8:20], refs[20:]
    bottoms, arrived, own_arrived, env_arrived = refs
    left, right = held[10:]
    channels, w = left.shape[1], left.shape[2]
    pieces = env_arrived.shape[1]
    deep = channels // pieces

    def env_copy(i, q):
        at = slice(q * deep, (q + 1) * deep)
        return pltpu.make_async_copy(given[10 + i].at[0, at], held[10 + i].at[0, at], env_arrived.at[i, q])

    copies = [
        pltpu.make_async_copy(source, target, arrived.at[index])
        for index, (source, target) in enumerate(zip(given[:10], held[:10]))
    ]
    own_copy = pltpu.make_async_copy(psi.at[0, 0], own, own_arrived)
    for copy in copies:
        copy.start()
    own_copy.start()
    for i in range(2):
        for q in range(pieces):
            env_copy(i, q).start()
    for k, tile in enumerate(near):
        stack_halves(tile, bottoms, k + 1)
    up_counts, up_block, up_top, up_bot, up_coef = held[:5]
    mv_counts, mv_src, mv_dst, mv_coef, energies = held[5:10]
    live = up_block.shape[2]
    me = lax.axis_index("tile")
    for copy in copies:
        copy.wait()
    channel = channel_row(up_counts, live, channels)
    plan_terms(
        channel * n + (up_top[0] ^ me), up_block[0] * n + (up_bot[0] ^ me), up_coef[0], up_ints, up_floats
    )
    channel = channel_row(mv_counts, live, channels)
    plan_terms(
        channel * n + (mv_dst[0] ^ me), channel * n + (mv_src[0] ^ me), mv_coef[0], mv_ints, mv_floats
    )
    at = lax.broadcasted_iota(jnp.int32, (1, live), 1)
    by_slot = jnp.zeros((1, live), F32)
    for k in range(n):
        by_slot += jnp.where(at == k, energies[0, k ^ me], 0.0)
    mv_floats[4:5] = by_slot
    own_copy.wait()
    stack_halves(own, bottoms, 0)
    for q in range(pieces):
        env_copy(0, q).wait()
        for c in range(q * deep, (q + 1) * deep):
            lefts[c * w : (c + 1) * w] = side_by_side(left[0, c])
    multiply_blocks(lefts, bottoms, up_entries, n, 0)
    for q in range(pieces):
        env_copy(1, q).wait()
        for c in range(q * deep, (q + 1) * deep):
            head, tail = heads_tails(right[0, c])
            rights[c, 0:w] = head
            rights[c, w : 2 * w] = tail


def prepare_call(n, psi, given, near):
    channels, w = given[-1].shape[1], given[-1].shape[2]
    live = given[1].shape[2]
    table = (8, live)
    return pl.pallas_call(
        functools.partial(prepare_kernel, n),
        out_shape=(
            jax.ShapeDtypeStruct((channels * w, 2 * w), BF16),
            jax.ShapeDtypeStruct((channels, 2 * w, w), BF16),
            jax.ShapeDtypeStruct(table, jnp.int32),
            jax.ShapeDtypeStruct(table, F32),
            jax.ShapeDtypeStruct(table, jnp.int32),
            jax.ShapeDtypeStruct(table, F32),
            jax.ShapeDtypeStruct((w, w), F32),
            pltpu.VMEM((2 * w + 1, w, w), F32),
        ),
        in_specs=[HBM] * (len(given) + 1) + [VMEM] * len(near),
        out_specs=(VMEM,) * 8,
        scratch_shapes=[
            *(
                pltpu.SMEM(x.shape, x.dtype) if x.shape[-1] in (channels, n) else pltpu.VMEM(x.shape, x.dtype)
                for x in given
            ),
            pltpu.VMEM((4 * w, n // 2 * w), BF16),
            pltpu.SemaphoreType.DMA((len(given) - 2,)),
            pltpu.SemaphoreType.DMA,
            pltpu.SemaphoreType.DMA((2, 4)),
        ],
        compiler_params=pltpu.CompilerParams(vmem_limit_bytes=14 << 20),
        cost_estimate=pl.CostEstimate(flops=10**9, bytes_accessed=6 << 20, transcendentals=0),
        name="prepare",
    )(*(pltpu.with_memory_space_constraint(x, pltpu.HBM) for x in (psi, *given)), *near)


def fetch_tables(sources, targets, arrived):
    copies = [
        pltpu.make_async_copy(source, target, arrived.at[index])
        for index, (source, target) in enumerate(zip(sources, targets))
    ]
    for copy in copies:
        copy.start()
    return copies


def renew_kernel(n, *refs):
    tiles = [refs[ORDER.index(k)] for k in range(n)]
    lefts, int_table, float_table, _, renewed, entries, bottoms, tops, ints, floats, arrived = refs[n:]
    channels, w = renewed.shape[0], renewed.shape[1]
    copies = fetch_tables((int_table, float_table), (ints, floats), arrived)
    for k in range(n // 2):
        stack_halves(tiles[n // 2 + k], bottoms, k)
    multiply_blocks(lefts, bottoms, entries, n, n // 2)
    for k in range(n):
        at = slice(k * w, (k + 1) * w)
        head, tail = heads_tails(tiles[k][...].T)
        tops[0:w, at] = head
        tops[w : 2 * w, at] = tail
    for copy in copies:
        copy.wait()
    spill(ints, floats, entries)

    def finish(g, unused):
        heads, tails = [], []
        for b in (2 * g, 2 * g + 1):
            pairs = [heads_tails(two_terms(ints, floats, entries, b * n + k)) for k in range(n)]
            heads.append(jnp.concatenate([pair[0] for pair in pairs], axis=0))
            tails.append(jnp.concatenate([pair[1] for pair in pairs], axis=0))
        small = product(tops[w:], jnp.concatenate(heads, axis=1))
        for i in range(2):
            b = 2 * g + i
            found = product(tops[0:w], jnp.concatenate([heads[i], tails[i]], axis=1))
            renewed[b] = found[:, :w] + (found[:, w:] + small[:, i * w : (i + 1) * w])
        return unused

    lax.fori_loop(0, channels // 2, finish, 0, unroll=4)


def renew_call(tiles, lefts, int_table, float_table, entries, channels):
    n, w = len(tiles), tiles[0].shape[0]
    return pl.pallas_call(
        functools.partial(renew_kernel, n),
        out_shape=(pltpu.VMEM((channels, w, w), F32), pltpu.VMEM(entries.shape, F32)),
        in_specs=[VMEM] * (n + 1) + [ANY] * 2 + [VMEM],
        out_specs=(VMEM, VMEM),
        input_output_aliases={n + 3: 1},
        scratch_shapes=[
            pltpu.VMEM((4 * w, n // 2 * w), BF16),
            pltpu.VMEM((2 * w, n * w), BF16),
            pltpu.SMEM(int_table.shape, jnp.int32),
            pltpu.SMEM(float_table.shape, F32),
            pltpu.SemaphoreType.DMA((2,)),
        ],
        compiler_params=pltpu.CompilerParams(vmem_limit_bytes=12 << 20),
        cost_estimate=pl.CostEstimate(flops=10**10, bytes_accessed=3 << 20, transcendentals=0),
        name="renew",
    )(
        *(tiles[k] for k in ORDER),
        lefts,
        int_table,
        float_table,
        pltpu.with_memory_space_constraint(entries, pltpu.VMEM),
    )[0]


def source_kernel(n, *refs):
    tiles = [refs[ORDER.index(k)] for k in range(n)]
    rights, int_table, float_table, entries, stats, sources, ints, floats, arrived = refs[n:]
    channels, w = rights.shape[0], rights.shape[2]
    copies = fetch_tables((int_table, float_table), (ints, floats), arrived)
    for k in range(n):
        at = slice(k * w, (k + 1) * w)
        head, tail = heads_tails(tiles[k][...])
        sources[at, 0:w] = head
        sources[at, w : 2 * w] = tail
        sources[at, 2 * w : 3 * w] = head
        sources[at, 3 * w : 4 * w] = tail
    group = channels // 2

    def multiply(g, unused):
        columns = []
        for h in range(group):
            value = rights[g * group + h]
            columns.append(jnp.concatenate([value[:w], value[:w], value[w:], value[w:]], axis=0))
        found = product(sources[...], jnp.concatenate(columns, axis=1))
        for h in range(group):
            for k in range(n):
                entries[(g * group + h) * n + k] = found[k * w : (k + 1) * w, h * w : (h + 1) * w]
        return unused

    lax.fori_loop(0, 2, multiply, 0, unroll=2)
    for copy in copies:
        copy.wait()
    spill(ints, floats, entries)
    weight = jnp.zeros((8, w), F32)
    energy = jnp.zeros((8, w), F32)
    for k in range(n):
        value = tiles[k][...]
        squares = jnp.sum((value * value).reshape(w // 8, 8, w), axis=0)
        weight += squares
        energy += floats[4, k] * squares
    stats[0:8] = weight
    stats[8:16] = energy
    stats[16:24] = jnp.full((8, w), floats[4, 0], F32)


def source_call(tiles, rights, int_table, float_table):
    n, w = len(tiles), rights.shape[2]
    return pl.pallas_call(
        functools.partial(source_kernel, n),
        out_shape=(
            pltpu.VMEM((2 * w + 1, w, w), F32),
            jax.ShapeDtypeStruct((24, w), F32),
        ),
        in_specs=[VMEM] * (n + 1) + [ANY] * 2,
        out_specs=(VMEM, VMEM),
        scratch_shapes=[
            pltpu.VMEM((n * w, 4 * w), BF16),
            pltpu.SMEM(int_table.shape, jnp.int32),
            pltpu.SMEM(float_table.shape, F32),
            pltpu.SemaphoreType.DMA((2,)),
        ],
        compiler_params=pltpu.CompilerParams(vmem_limit_bytes=12 << 20),
        cost_estimate=pl.CostEstimate(flops=10**10, bytes_accessed=10 << 20, transcendentals=0),
        name="sources",
    )(*(tiles[k] for k in ORDER), rights, int_table, float_table)


def apply_kernel(n, *refs):
    tiles = [refs[ORDER.index(k)] for k in range(n)]
    own, received, entries, int_table, float_table = refs[n : n + 5]
    outs = refs[n + 5 : 2 * n + 5]
    lefts, ints, floats, arrived = refs[2 * n + 5 :]
    channels, w = own.shape[0], own.shape[1]
    copies = fetch_tables((int_table, float_table), (ints, floats), arrived)
    leading = lax.axis_index("seg") == 0

    def halve(env):
        for c in range(channels):
            head, tail = heads_tails(env[c])
            lefts[0:w, c * w : (c + 1) * w] = head
            lefts[w : 2 * w, c * w : (c + 1) * w] = tail

    @pl.when(leading)
    def _():
        halve(own)

    @pl.when(jnp.logical_not(leading))
    def _():
        halve(received)

    for copy in copies:
        copy.wait()
    inner = jnp.zeros((8, w), F32)
    for k in range(0, n, 2):
        heads, tails = [], []
        for t in (k, k + 1):
            pairs = [
                heads_tails(two_terms(ints, floats, entries, c * n + t)) for c in range(channels)
            ]
            heads.append(jnp.concatenate([pair[0] for pair in pairs], axis=0))
            tails.append(jnp.concatenate([pair[1] for pair in pairs], axis=0))
        small = product(lefts[w:], jnp.concatenate(heads, axis=1))
        for i in range(2):
            found = product(lefts[0:w], jnp.concatenate([heads[i], tails[i]], axis=1))
            value = found[:, :w] + (found[:, w:] + small[:, i * w : (i + 1) * w])
            outs[k + i][0:w] = value
            inner += jnp.sum((value * tiles[k + i][...]).reshape(w // 8, 8, w), axis=0)
    for k in range(n):
        outs[k][w : w + 8] = inner


def apply_call(tiles, own, received, entries, int_table, float_table):
    n, w = len(tiles), own.shape[1]
    return pl.pallas_call(
        functools.partial(apply_kernel, n),
        out_shape=tuple(jax.ShapeDtypeStruct((w + 8, w), F32) for _ in range(n)),
        in_specs=[VMEM] * (n + 3) + [ANY] * 2,
        out_specs=(VMEM,) * n,
        scratch_shapes=[
            pltpu.VMEM((2 * w, own.shape[0] * w), BF16),
            pltpu.SMEM(int_table.shape, jnp.int32),
            pltpu.SMEM(float_table.shape, F32),
            pltpu.SemaphoreType.DMA((2,)),
        ],
        compiler_params=pltpu.CompilerParams(vmem_limit_bytes=12 << 20),
        cost_estimate=pl.CostEstimate(flops=5 * 10**9, bytes_accessed=10 << 20, transcendentals=0),
        name="applied",
    )(
        *(tiles[k] for k in ORDER),
        own,
        received,
        pltpu.with_memory_space_constraint(entries, pltpu.VMEM),
        int_table,
        float_table,
    )


def finish_kernel(*refs):
    parts = refs[:-4]
    own, stats, residual, quotient = refs[-4:]
    w = own.shape[0]
    total = parts[0][...]
    for part in parts[1:]:
        total = total + part[...]
    value = own[...]
    numerator = jnp.sum(total[w : w + 8]) + jnp.sum(stats[8:16])
    ratio = jnp.full((1, 128), numerator, F32) / jnp.full((1, 128), jnp.sum(stats[0:8]), F32)
    residual[...] = total[:w] + (stats[16:17] - ratio) * value
    quotient[...] = ratio


def finish_call(parts, own, stats):
    w = own.shape[0]
    return pl.pallas_call(
        finish_kernel,
        out_shape=(jax.ShapeDtypeStruct((w, w), F32), jax.ShapeDtypeStruct((1, 128), F32)),
        in_specs=[VMEM] * (len(parts) + 2),
        out_specs=(VMEM, VMEM),
        compiler_params=pltpu.CompilerParams(vmem_limit_bytes=2 << 20),
        name="finish",
    )(*parts, own, stats)


def shards(
    psi,
    left_env,
    right_env,
    site_energy,
    mv_counts,
    mv_src,
    mv_dst,
    mv_coef,
    up_counts,
    up_block,
    up_top,
    up_bot,
    up_coef,
):
    n = lax.axis_size("tile")
    def across(value, k):
        return lax.ppermute(value, "tile", [(i, i ^ k) for i in range(n)])

    own = psi[0, 0]
    half = n // 2
    tiles = {k: across(own, k) for k in range(1, half + 1)}
    for k in range(1, half):
        tiles[half + k] = across(tiles[half], k)

    given = [up_counts, up_block, up_top, up_bot, up_coef, mv_counts, mv_src, mv_dst, mv_coef, site_energy]
    lefts, rights, up_ints, up_floats, mv_ints, mv_floats, own, products = prepare_call(
        n, psi, [*given, left_env, right_env], [tiles[k] for k in range(1, half)]
    )
    tiles[0] = own
    tiles = [tiles[k] for k in range(n)]
    renewal = renew_call(tiles, lefts, up_ints, up_floats, products, left_env.shape[1])
    received = lax.ppermute(renewal, "seg", [(0, 1), (1, 0)])
    entries, stats = source_call(tiles, rights, mv_ints, mv_floats)
    partials = apply_call(tiles, left_env[0], received, entries, mv_ints, mv_floats)

    far = partials[half]
    for k in range(half - 1, 0, -1):
        far = far + across(partials[half + k], k)
    far = across(far, half)
    parts = [partials[0], *(across(partials[k], k) for k in range(half - 1, 0, -1)), far]
    residual, quotient = finish_call(parts, own, stats)
    return (residual[None, None], renewal[None], quotient[0, :1])


def solution(mesh):
    per_run = P(("parts", "seg"), "tile", None)
    return jax.shard_map(
        shards if mesh.shape["tile"] == 8 else general_shards,
        mesh=mesh,
        in_specs=(
            P(("parts", "seg"), "tile", None, None),
            P(("parts", "seg"), "tile", None, None),
            P(("parts", "seg"), "tile", None, None),
            P(("parts", "seg"), None),
            per_run,
            per_run,
            per_run,
            per_run,
            per_run,
            per_run,
            per_run,
            per_run,
            per_run,
        ),
        out_specs=(
            P(("parts", "seg"), "tile", None, None),
            P(("parts", "seg"), "tile", None, None),
            P(("parts", "seg")),
        ),
        check_vma=False,
    )
```

```python
import functools

import jax
import jax.numpy as jnp
from jax import lax
from jax.experimental import pallas as pl
from jax.experimental.pallas import tpu as pltpu
from jax.sharding import PartitionSpec as P

MAXT = 24
ORDER = (0, 7, 6, 5, 4, 1, 2, 3)
F32 = jnp.float32
BF16 = jnp.bfloat16
VMEM = pl.BlockSpec(memory_space=pltpu.VMEM)
SMEM = pl.BlockSpec(memory_space=pltpu.SMEM)
ANY = pl.BlockSpec(memory_space=pl.ANY)
HBM = pl.BlockSpec(memory_space=pltpu.HBM)


def passed_along(value, axis, steps):
    count = lax.axis_size(axis)
    first, last = (max(0, -steps), min(count, count - steps))
    return lax.ppermute(value, axis, [(source, source + steps) for source in range(first, last)])


def slot_layout(counts, most):
    block_ends = jnp.cumsum(counts)
    block_starts = block_ends - counts
    slots = jnp.arange(most, dtype=jnp.int32)
    live_slot = slots[None, :] < counts[:, None]
    slot_pos = jnp.where(live_slot, block_starts[:, None] + slots[None, :], 0)
    return (slot_pos, live_slot)


def apply_terms(gathered, env_used, right_own, counts, sources, targets, coefs):
    psi_count = gathered.shape[0]
    tile_width = gathered.shape[1]
    channels = counts.shape[0]
    quarter = channels // 4
    slot_pos, live_slot = slot_layout(counts, MAXT)
    src_slots = sources[slot_pos]
    dst_slots = targets[slot_pos]
    coef_slots = jnp.where(live_slot, coefs[slot_pos], 0.0)

    def apply_one_turn(running, inputs):
        env_part, right_part, src_part, dst_part, coef_part = inputs
        inner = jnp.einsum(
            "csij,cjk->csik", gathered[src_part], right_part, precision=lax.Precision.HIGHEST
        )
        contrib = jnp.einsum("cij,csjk->csik", env_part, inner, precision=lax.Precision.HIGHEST)
        contrib = contrib * coef_part[:, :, None, None]
        added = jax.ops.segment_sum(
            contrib.reshape(-1, tile_width, tile_width),
            dst_part.reshape(-1),
            num_segments=psi_count,
        )
        return (running + added, None)

    inputs = (
        env_used.reshape(4, quarter, tile_width, tile_width),
        right_own.reshape(4, quarter, tile_width, tile_width),
        src_slots.reshape(4, quarter, MAXT),
        dst_slots.reshape(4, quarter, MAXT),
        coef_slots.reshape(4, quarter, MAXT),
    )
    start_sum = jnp.zeros((psi_count, tile_width, tile_width), jnp.float32)
    summed, unused = lax.scan(apply_one_turn, start_sum, inputs)
    return summed


def renew_env(gathered, own_env, counts, blocks, tops, bottoms, coefs):
    tile_width = gathered.shape[1]
    channels = counts.shape[0]
    quarter = channels // 4
    slot_pos, live_slot = slot_layout(counts, MAXT)
    block_slots = blocks[slot_pos]
    top_slots = tops[slot_pos]
    bottom_slots = bottoms[slot_pos]
    coef_slots = jnp.where(live_slot, coefs[slot_pos], 0.0)

    def renew_one_turn(inputs):
        block_part, top_part, bottom_part, coef_part = inputs
        inner = jnp.einsum(
            "csij,csjk->csik",
            own_env[block_part],
            gathered[bottom_part],
            precision=lax.Precision.HIGHEST,
        )
        contrib = jnp.einsum(
            "csji,csjk->csik", gathered[top_part], inner, precision=lax.Precision.HIGHEST
        )
        contrib = contrib * coef_part[:, :, None, None]
        return jnp.sum(contrib, axis=1)

    inputs = (
        block_slots.reshape(4, quarter, MAXT),
        top_slots.reshape(4, quarter, MAXT),
        bottom_slots.reshape(4, quarter, MAXT),
        coef_slots.reshape(4, quarter, MAXT),
    )
    stacked = lax.map(renew_one_turn, inputs)
    return stacked.reshape(channels, tile_width, tile_width)


def general_shards(
    psi,
    left_env,
    right_env,
    site_energy,
    mv_counts,
    mv_src,
    mv_dst,
    mv_coef,
    up_counts,
    up_block,
    up_top,
    up_bot,
    up_coef,
):
    own_psi = psi[0]
    own_env = left_env[0]
    gathered = lax.all_gather(own_psi, "tile", axis=0, tiled=True)
    renewal = renew_env(
        gathered,
        own_env,
        up_counts[0, 0],
        up_block[0, 0],
        up_top[0, 0],
        up_bot[0, 0],
        up_coef[0, 0],
    )
    received = passed_along(renewal, "seg", 1)
    leading = lax.axis_index("seg") == 0
    env_used = jnp.where(leading, own_env, received)
    partial_value = apply_terms(
        gathered, env_used, right_env[0], mv_counts[0, 0], mv_src[0, 0], mv_dst[0, 0], mv_coef[0, 0]
    )
    row_count = own_psi.shape[0]
    energies = site_energy[0]
    row_start = lax.axis_index("tile") * row_count
    summed_own = lax.psum_scatter(partial_value, "tile", scatter_dimension=0, tiled=True)
    own_energy = lax.dynamic_slice_in_dim(energies, row_start, row_count, 0)
    own_rows = summed_own + own_energy[:, None, None] * own_psi
    numerator = lax.psum(jnp.sum(own_psi * own_rows), "tile")
    denominator = jnp.sum(gathered * gathered)
    quotient = numerator / denominator
    residual = own_rows - quotient * own_psi
    return (residual[None], renewal[None], jnp.reshape(quotient, (1,)))


def heads_tails(value):
    head = value.astype(BF16)
    return head, (value - head.astype(F32)).astype(BF16)


def side_by_side(value):
    return jnp.concatenate(heads_tails(value), axis=1)


def product(left, right):
    return jnp.dot(left, right, preferred_element_type=F32)


def channel_row(counts, live, channels):
    at = lax.broadcasted_iota(jnp.int32, (1, live), 1)
    found = jnp.zeros((1, live), jnp.int32)
    end = 0
    for c in range(channels):
        end = end + counts[0, 0, c]
        found += (at >= end).astype(jnp.int32)
    return found


def thirds(value):
    first = value.astype(BF16)
    value = value - first.astype(F32)
    second = value.astype(BF16)
    return [first.astype(F32), second.astype(F32), value - second.astype(F32)]


def over_entries(rows, chosen):
    return lax.dot_general(
        rows.astype(BF16), chosen, (((1,), (1,)), ((), ())), preferred_element_type=F32
    )


def plan_terms(group, source, coef, ints, floats):
    w, live = 128, group.shape[1]
    groups = lax.broadcasted_iota(jnp.int32, (w, live), 0)
    member = group == groups
    ones = jnp.where(member, 1.0, 0.0)
    earlier = lax.broadcasted_iota(jnp.int32, (live, live), 0) < lax.broadcasted_iota(
        jnp.int32, (live, live), 1
    )
    earlier = jnp.where(earlier, 1.0, 0.0).astype(BF16)
    before = product(ones.astype(BF16), earlier)
    size = jnp.sum(ones, axis=1, keepdims=True)
    rank = jnp.sum(ones * before, axis=0, keepdims=True)
    size_here = jnp.sum(ones * size, axis=0, keepdims=True)
    spilled = jnp.where(size_here > 2.0, jnp.where(rank > 0.0, 1.0, 0.0), 0.0)
    parts = thirds(coef)
    sources = source.astype(F32)
    zero = jnp.zeros_like(coef)
    rows = jnp.concatenate([sources, *parts, ones[0:1] * 0.0 + 1.0, zero, zero, zero], axis=0)
    first = over_entries(rows, jnp.where(before == 0.0, ones, 0.0).astype(BF16))
    second = over_entries(rows, jnp.where(before == 1.0, ones, 0.0).astype(BF16))
    large = over_entries(rows, ones.astype(BF16))[4:5] > 2.0
    at = lax.broadcasted_iota(jnp.int32, (1, w), 1)
    ints[0:1, 0:w] = first[0:1].astype(jnp.int32)
    ints[1:2, 0:w] = jnp.where(large, w + at, second[0:1].astype(jnp.int32))
    floats[0:1, 0:w] = first[1:2] + first[2:3] + first[3:4]
    floats[1:2, 0:w] = jnp.where(large, 1.0, second[1:2] + second[2:3] + second[3:4])

    twos = jnp.where(size > 2.0, jnp.floor(size * 0.5), 0.0)
    column = lax.broadcasted_iota(jnp.int32, (w, w), 0)
    lower = jnp.where(lax.broadcasted_iota(jnp.int32, (w, w), 1) < column, 1.0, 0.0).astype(BF16)
    start = product(lower, jnp.broadcast_to(twos, (w, w)).astype(BF16))[:, 0:1]
    count = jnp.sum(twos)
    two = jnp.floor((rank - 1.0) * 0.5)
    second = rank - 1.0 - 2.0 * two
    place = jnp.sum(ones * start, axis=0, keepdims=True) + two
    place = jnp.where(spilled > 0.0, place, -1.0)
    column = lax.broadcasted_iota(jnp.int32, (live, live), 0).astype(F32)
    chosen = jnp.where(place == column, 1.0, 0.0)
    again = jnp.where(two > 0.0, 1.0, 0.0)
    rows = jnp.concatenate(
        [sources, *parts, (group + w).astype(F32), again, zero, zero], axis=0
    )
    past = lax.broadcasted_iota(jnp.int32, (1, live), 1).astype(F32) >= count
    for i in range(2):
        listed = over_entries(rows, (chosen * jnp.where(second == i, 1.0, 0.0)).astype(BF16))
        ints[2 + i : 3 + i] = listed[0:1].astype(jnp.int32)
        floats[2 + i : 3 + i] = listed[1:2] + listed[2:3] + listed[3:4]
        if i == 0:
            ints[4:5] = jnp.where(past, 2 * w, listed[4:5].astype(jnp.int32))
            floats[5:6] = listed[5:6]
    ints[5:6] = jnp.full((1, live), count).astype(jnp.int32)


def spill(ints, floats, blocks):
    def add(q):
        to = ints[4, q]
        held = jnp.where(floats[5, q] > 0.0, blocks[to], 0.0)
        pair = floats[2, q] * blocks[ints[2, q]] + floats[3, q] * blocks[ints[3, q]]
        blocks[to] = held + pair

    def four(q, unused):
        for i in range(4):
            add(4 * q + i)
        return unused

    lax.fori_loop(0, lax.div(ints[5, 0] + 3, 4), four, 0)


def two_terms(ints, floats, blocks, g):
    return floats[0, g] * blocks[ints[0, g]] + floats[1, g] * blocks[ints[1, g]]


def stack_halves(tile, stacked, k):
    w = tile.shape[0]
    at = slice(k * w, (k + 1) * w)
    head, tail = heads_tails(tile[...])
    stacked[0:w, at] = head
    stacked[w : 2 * w, at] = head
    stacked[2 * w : 3 * w, at] = tail
    stacked[3 * w : 4 * w, at] = tail


def multiply_blocks(lefts, stacked, entries, n, first, parts=2):
    w = lefts.shape[1] // 2
    count = stacked.shape[1] // w
    group = lefts.shape[0] // w // parts

    def multiply(g, unused):
        own = lefts[pl.ds(pl.multiple_of(g * (group * w), group * w), group * w)]
        found = product(jnp.concatenate([own, own], axis=1), stacked[...])
        for h in range(group):
            for k in range(count):
                entries[(g * group + h) * n + first + k] = found[
                    h * w : (h + 1) * w, k * w : (k + 1) * w
                ]
        return unused

    lax.fori_loop(0, parts, multiply, 0, unroll=parts)


def prepare_kernel(n, *refs):
    psi, given, refs = refs[0], refs[1:13], refs[13:]
    near, refs = refs[: n // 2 - 1], refs[n // 2 - 1 :]
    lefts, rights, up_ints, up_floats, mv_ints, mv_floats, own, up_entries = refs[:8]
    held, refs = refs[8:20], refs[20:]
    bottoms, arrived, own_arrived, env_arrived = refs
    left, right = held[10:]
    channels, w = left.shape[1], left.shape[2]
    pieces = env_arrived.shape[1]
    deep = channels // pieces

    def env_copy(i, q):
        at = slice(q * deep, (q + 1) * deep)
        return pltpu.make_async_copy(given[10 + i].at[0, at], held[10 + i].at[0, at], env_arrived.at[i, q])

    copies = [
        pltpu.make_async_copy(source, target, arrived.at[index])
        for index, (source, target) in enumerate(zip(given[:10], held[:10]))
    ]
    own_copy = pltpu.make_async_copy(psi.at[0, 0], own, own_arrived)
    for copy in copies:
        copy.start()
    own_copy.start()
    for i in range(2):
        for q in range(pieces):
            env_copy(i, q).start()
    for k, tile in enumerate(near):
        stack_halves(tile, bottoms, k + 1)
    up_counts, up_block, up_top, up_bot, up_coef = held[:5]
    mv_counts, mv_src, mv_dst, mv_coef, energies = held[5:10]
    live = up_block.shape[2]
    me = lax.axis_index("tile")
    for copy in copies:
        copy.wait()
    channel = channel_row(up_counts, live, channels)
    plan_terms(
        channel * n + (up_top[0] ^ me), up_block[0] * n + (up_bot[0] ^ me), up_coef[0], up_ints, up_floats
    )
    channel = channel_row(mv_counts, live, channels)
    plan_terms(
        channel * n + (mv_dst[0] ^ me), channel * n + (mv_src[0] ^ me), mv_coef[0], mv_ints, mv_floats
    )
    at = lax.broadcasted_iota(jnp.int32, (1, live), 1)
    by_slot = jnp.zeros((1, live), F32)
    for k in range(n):
        by_slot += jnp.where(at == k, energies[0, k ^ me], 0.0)
    mv_floats[4:5] = by_slot
    own_copy.wait()
    stack_halves(own, bottoms, 0)
    for q in range(pieces):
        env_copy(0, q).wait()
        for c in range(q * deep, (q + 1) * deep):
            lefts[c * w : (c + 1) * w] = side_by_side(left[0, c])
    multiply_blocks(lefts, bottoms, up_entries, n, 0)
    for q in range(pieces):
        env_copy(1, q).wait()
        for c in range(q * deep, (q + 1) * deep):
            head, tail = heads_tails(right[0, c])
            rights[c, 0:w] = head
            rights[c, w : 2 * w] = tail


def prepare_call(n, psi, given, near):
    channels, w = given[-1].shape[1], given[-1].shape[2]
    live = given[1].shape[2]
    table = (8, live)
    return pl.pallas_call(
        functools.partial(prepare_kernel, n),
        out_shape=(
            jax.ShapeDtypeStruct((channels * w, 2 * w), BF16),
            jax.ShapeDtypeStruct((channels, 2 * w, w), BF16),
            jax.ShapeDtypeStruct(table, jnp.int32),
            jax.ShapeDtypeStruct(table, F32),
            jax.ShapeDtypeStruct(table, jnp.int32),
            jax.ShapeDtypeStruct(table, F32),
            jax.ShapeDtypeStruct((w, w), F32),
            pltpu.VMEM((2 * w + 1, w, w), F32),
        ),
        in_specs=[HBM] * (len(given) + 1) + [VMEM] * len(near),
        out_specs=(VMEM,) * 8,
        scratch_shapes=[
            *(
                pltpu.SMEM(x.shape, x.dtype) if x.shape[-1] in (channels, n) else pltpu.VMEM(x.shape, x.dtype)
                for x in given
            ),
            pltpu.VMEM((4 * w, n // 2 * w), BF16),
            pltpu.SemaphoreType.DMA((len(given) - 2,)),
            pltpu.SemaphoreType.DMA,
            pltpu.SemaphoreType.DMA((2, 4)),
        ],
        compiler_params=pltpu.CompilerParams(vmem_limit_bytes=14 << 20),
        cost_estimate=pl.CostEstimate(flops=10**9, bytes_accessed=6 << 20, transcendentals=0),
        name="prepare",
    )(*(pltpu.with_memory_space_constraint(x, pltpu.HBM) for x in (psi, *given)), *near)


def fetch_tables(sources, targets, arrived):
    copies = [
        pltpu.make_async_copy(source, target, arrived.at[index])
        for index, (source, target) in enumerate(zip(sources, targets))
    ]
    for copy in copies:
        copy.start()
    return copies


def renew_kernel(n, *refs):
    tiles = [refs[ORDER.index(k)] for k in range(n)]
    lefts, int_table, float_table, _, renewed, entries, bottoms, tops, ints, floats, arrived = refs[n:]
    channels, w = renewed.shape[0], renewed.shape[1]
    copies = fetch_tables((int_table, float_table), (ints, floats), arrived)
    for k in range(n // 2):
        stack_halves(tiles[n // 2 + k], bottoms, k)
    multiply_blocks(lefts, bottoms, entries, n, n // 2)
    for k in range(n):
        at = slice(k * w, (k + 1) * w)
        head, tail = heads_tails(tiles[k][...].T)
        tops[0:w, at] = head
        tops[w : 2 * w, at] = tail
    for copy in copies:
        copy.wait()
    spill(ints, floats, entries)

    def finish(g, unused):
        heads, tails = [], []
        for b in (2 * g, 2 * g + 1):
            pairs = [heads_tails(two_terms(ints, floats, entries, b * n + k)) for k in range(n)]
            heads.append(jnp.concatenate([pair[0] for pair in pairs], axis=0))
            tails.append(jnp.concatenate([pair[1] for pair in pairs], axis=0))
        small = product(tops[w:], jnp.concatenate(heads, axis=1))
        for i in range(2):
            b = 2 * g + i
            found = product(tops[0:w], jnp.concatenate([heads[i], tails[i]], axis=1))
            renewed[b] = found[:, :w] + (found[:, w:] + small[:, i * w : (i + 1) * w])
        return unused

    lax.fori_loop(0, channels // 2, finish, 0, unroll=8)


def renew_call(tiles, lefts, int_table, float_table, entries, channels):
    n, w = len(tiles), tiles[0].shape[0]
    return pl.pallas_call(
        functools.partial(renew_kernel, n),
        out_shape=(pltpu.VMEM((channels, w, w), F32), pltpu.VMEM(entries.shape, F32)),
        in_specs=[VMEM] * (n + 1) + [ANY] * 2 + [VMEM],
        out_specs=(VMEM, VMEM),
        input_output_aliases={n + 3: 1},
        scratch_shapes=[
            pltpu.VMEM((4 * w, n // 2 * w), BF16),
            pltpu.VMEM((2 * w, n * w), BF16),
            pltpu.SMEM(int_table.shape, jnp.int32),
            pltpu.SMEM(float_table.shape, F32),
            pltpu.SemaphoreType.DMA((2,)),
        ],
        compiler_params=pltpu.CompilerParams(vmem_limit_bytes=12 << 20),
        cost_estimate=pl.CostEstimate(flops=10**10, bytes_accessed=3 << 20, transcendentals=0),
        name="renew",
    )(
        *(tiles[k] for k in ORDER),
        lefts,
        int_table,
        float_table,
        pltpu.with_memory_space_constraint(entries, pltpu.VMEM),
    )[0]


def source_kernel(n, *refs):
    tiles = [refs[ORDER.index(k)] for k in range(n)]
    rights, int_table, float_table, entries, sources, ints, floats, arrived = refs[n:]
    channels, w = rights.shape[0], rights.shape[2]
    copies = fetch_tables((int_table, float_table), (ints, floats), arrived)
    for k in range(n):
        at = slice(k * w, (k + 1) * w)
        head, tail = heads_tails(tiles[k][...])
        sources[at, 0:w] = head
        sources[at, w : 2 * w] = tail
        sources[at, 2 * w : 3 * w] = head
        sources[at, 3 * w : 4 * w] = tail
    group = channels // 2

    def multiply(g, unused):
        columns = []
        for h in range(group):
            value = rights[g * group + h]
            columns.append(jnp.concatenate([value[:w], value[:w], value[w:], value[w:]], axis=0))
        found = product(sources[...], jnp.concatenate(columns, axis=1))
        for h in range(group):
            for k in range(n):
                entries[(g * group + h) * n + k] = found[k * w : (k + 1) * w, h * w : (h + 1) * w]
        return unused

    lax.fori_loop(0, 2, multiply, 0, unroll=2)
    for copy in copies:
        copy.wait()
    spill(ints, floats, entries)


def source_call(tiles, rights, int_table, float_table):
    n, w = len(tiles), rights.shape[2]
    return pl.pallas_call(
        functools.partial(source_kernel, n),
        out_shape=pltpu.VMEM((2 * w + 1, w, w), F32),
        in_specs=[VMEM] * (n + 1) + [ANY] * 2,
        out_specs=VMEM,
        scratch_shapes=[
            pltpu.VMEM((n * w, 4 * w), BF16),
            pltpu.SMEM(int_table.shape, jnp.int32),
            pltpu.SMEM(float_table.shape, F32),
            pltpu.SemaphoreType.DMA((2,)),
        ],
        compiler_params=pltpu.CompilerParams(vmem_limit_bytes=12 << 20),
        cost_estimate=pl.CostEstimate(flops=10**10, bytes_accessed=10 << 20, transcendentals=0),
        name="sources",
    )(*(tiles[k] for k in ORDER), rights, int_table, float_table)


def norm_kernel(n, *refs):
    tiles, (floats, stats) = refs[:n], refs[n:]
    w = stats.shape[1]
    weight = jnp.zeros((8, w), F32)
    energy = jnp.zeros((8, w), F32)
    for k in range(n):
        value = tiles[k][...]
        squares = jnp.sum((value * value).reshape(w // 8, 8, w), axis=0)
        weight += squares
        energy += floats[4:5, k : k + 1] * squares
    stats[0:8] = weight
    stats[8:16] = energy
    stats[16:24] = jnp.broadcast_to(floats[4:5, 0:1], (8, w))


def norm_call(tiles, float_table):
    n, w = len(tiles), tiles[0].shape[0]
    return pl.pallas_call(
        functools.partial(norm_kernel, n),
        out_shape=jax.ShapeDtypeStruct((24, w), F32),
        in_specs=[VMEM] * (n + 1),
        out_specs=VMEM,
        compiler_params=pltpu.CompilerParams(vmem_limit_bytes=2 << 20),
        name="norms",
    )(*tiles, float_table)


def apply_kernel(n, *refs):
    tiles = [refs[ORDER.index(k)] for k in range(n)]
    own, received, entries, int_table, float_table = refs[n : n + 5]
    outs = refs[n + 5 : 2 * n + 5]
    lefts, ints, floats, arrived = refs[2 * n + 5 :]
    channels, w = own.shape[0], own.shape[1]
    copies = fetch_tables((int_table, float_table), (ints, floats), arrived)
    leading = lax.axis_index("seg") == 0

    def halve(env):
        for c in range(channels):
            head, tail = heads_tails(env[c])
            lefts[0:w, c * w : (c + 1) * w] = head
            lefts[w : 2 * w, c * w : (c + 1) * w] = tail

    @pl.when(leading)
    def _():
        halve(own)

    @pl.when(jnp.logical_not(leading))
    def _():
        halve(received)

    for copy in copies:
        copy.wait()
    inner = jnp.zeros((8, w), F32)
    for k in range(0, n, 2):
        heads, tails = [], []
        for t in (k, k + 1):
            pairs = [
                heads_tails(two_terms(ints, floats, entries, c * n + t)) for c in range(channels)
            ]
            heads.append(jnp.concatenate([pair[0] for pair in pairs], axis=0))
            tails.append(jnp.concatenate([pair[1] for pair in pairs], axis=0))
        small = product(lefts[w:], jnp.concatenate(heads, axis=1))
        for i in range(2):
            found = product(lefts[0:w], jnp.concatenate([heads[i], tails[i]], axis=1))
            value = found[:, :w] + (found[:, w:] + small[:, i * w : (i + 1) * w])
            outs[k + i][0:w] = value
            inner += jnp.sum((value * tiles[k + i][...]).reshape(w // 8, 8, w), axis=0)
    for k in range(n):
        outs[k][w : w + 8] = inner


def apply_call(tiles, own, received, entries, int_table, float_table):
    n, w = len(tiles), own.shape[1]
    return pl.pallas_call(
        functools.partial(apply_kernel, n),
        out_shape=tuple(jax.ShapeDtypeStruct((w + 8, w), F32) for _ in range(n)),
        in_specs=[VMEM] * (n + 3) + [ANY] * 2,
        out_specs=(VMEM,) * n,
        scratch_shapes=[
            pltpu.VMEM((2 * w, own.shape[0] * w), BF16),
            pltpu.SMEM(int_table.shape, jnp.int32),
            pltpu.SMEM(float_table.shape, F32),
            pltpu.SemaphoreType.DMA((2,)),
        ],
        compiler_params=pltpu.CompilerParams(vmem_limit_bytes=12 << 20),
        cost_estimate=pl.CostEstimate(flops=5 * 10**9, bytes_accessed=10 << 20, transcendentals=0),
        name="applied",
    )(
        *(tiles[k] for k in ORDER),
        own,
        received,
        pltpu.with_memory_space_constraint(entries, pltpu.VMEM),
        int_table,
        float_table,
    )


def finish_kernel(*refs):
    parts = refs[:-4]
    own, stats, residual, quotient = refs[-4:]
    w = own.shape[0]
    total = parts[0][...]
    for part in parts[1:]:
        total = total + part[...]
    value = own[...]
    numerator = jnp.sum(total[w : w + 8]) + jnp.sum(stats[8:16])
    ratio = jnp.full((1, 128), numerator, F32) / jnp.full((1, 128), jnp.sum(stats[0:8]), F32)
    residual[...] = total[:w] + (stats[16:17] - ratio) * value
    quotient[...] = ratio


def finish_call(parts, own, stats):
    w = own.shape[0]
    return pl.pallas_call(
        finish_kernel,
        out_shape=(jax.ShapeDtypeStruct((w, w), F32), jax.ShapeDtypeStruct((1, 128), F32)),
        in_specs=[VMEM] * (len(parts) + 2),
        out_specs=(VMEM, VMEM),
        compiler_params=pltpu.CompilerParams(vmem_limit_bytes=2 << 20),
        name="finish",
    )(*parts, own, stats)


def shards(
    psi,
    left_env,
    right_env,
    site_energy,
    mv_counts,
    mv_src,
    mv_dst,
    mv_coef,
    up_counts,
    up_block,
    up_top,
    up_bot,
    up_coef,
):
    n = lax.axis_size("tile")
    def across(value, k):
        return lax.ppermute(value, "tile", [(i, i ^ k) for i in range(n)])

    own = psi[0, 0]
    half = n // 2
    tiles = {k: across(own, k) for k in range(1, half + 1)}
    for k in range(1, half):
        tiles[half + k] = across(tiles[half], k)

    given = [up_counts, up_block, up_top, up_bot, up_coef, mv_counts, mv_src, mv_dst, mv_coef, site_energy]
    lefts, rights, up_ints, up_floats, mv_ints, mv_floats, own, products = prepare_call(
        n, psi, [*given, left_env, right_env], [tiles[k] for k in range(1, half)]
    )
    tiles[0] = own
    tiles = [tiles[k] for k in range(n)]
    renewal = renew_call(tiles, lefts, up_ints, up_floats, products, left_env.shape[1])
    received = lax.ppermute(renewal, "seg", [(0, 1), (1, 0)])
    entries = source_call(tiles, rights, mv_ints, mv_floats)
    stats = norm_call(tiles, mv_floats)
    partials = apply_call(tiles, left_env[0], received, entries, mv_ints, mv_floats)

    far = partials[half]
    for k in range(half - 1, 0, -1):
        far = far + across(partials[half + k], k)
    far = across(far, half)
    parts = [partials[0], *(across(partials[k], k) for k in range(half - 1, 0, -1)), far]
    residual, quotient = finish_call(parts, own, stats)
    return (residual[None, None], renewal[None], quotient[0, :1])


def solution(mesh):
    per_run = P(("parts", "seg"), "tile", None)
    return jax.shard_map(
        shards if mesh.shape["tile"] == 8 else general_shards,
        mesh=mesh,
        in_specs=(
            P(("parts", "seg"), "tile", None, None),
            P(("parts", "seg"), "tile", None, None),
            P(("parts", "seg"), "tile", None, None),
            P(("parts", "seg"), None),
            per_run,
            per_run,
            per_run,
            per_run,
            per_run,
            per_run,
            per_run,
            per_run,
            per_run,
        ),
        out_specs=(
            P(("parts", "seg"), "tile", None, None),
            P(("parts", "seg"), "tile", None, None),
            P(("parts", "seg")),
        ),
        check_vma=False,
    )
```
